128 devices in a mesh: oct: 4 (over y), box: 32 (over z, x, core).
Axes of the slice: x: 4, y: 4, z: 4, core: 2. Of those that a mesh axis runs over, the one named last changes fastest.
Arguments:
- coarse_multipole: bfloat16 [64, 8192], P(None, ('oct', 'box')), may hold values from -6 to 6
- fine_multipole: bfloat16 [64, 65536], P(None, ('oct', 'box')), may hold values from -6 to 6
- parent_local: float32 [64, 8192], P(None, ('oct', 'box')), may hold values from -4 to 4
- operators: bfloat16 [316, 64, 64], replicated, may hold values from -0.09375 to 0.09375
- child_maps: bfloat16 [8, 64, 64], replicated, may hold values from -0.75 to 0.75
- coarse_near_boxes: int32 [131072, 2], P(('oct', 'box')), may hold values from 0 to 63
- coarse_near_shift: int32 [131072], P(('oct', 'box')), may hold values from 0 to 315, as said below
- coarse_far_boxes: int32 [65536, 2], P(('oct', 'box')), may hold values from 0 to 63
- coarse_far_owner: int32 [65536, 1], P(('oct', 'box')), may hold values from 0 to 127, as said below
- coarse_far_shift: int32 [65536], P(('oct', 'box')), may hold values from 0 to 315, as said below
- fine_near_boxes: int32 [1048576, 2], P(('oct', 'box')), may hold values from 0 to 511
- fine_near_shift: int32 [1048576], P(('oct', 'box')), may hold values from 0 to 315, as said below
- fine_far_boxes: int32 [262144, 2], P(('oct', 'box')), may hold values from 0 to 511
- fine_far_owner: int32 [262144, 1], P(('oct', 'box')), may hold values from 0 to 127, as said below
- fine_far_shift: int32 [262144], P(('oct', 'box')), may hold values from 0 to 315, as said below
Outputs:
- coarse_local: bfloat16 [64, 8192], P(None, ('oct', 'box'))
- fine_local: bfloat16 [64, 65536], P(None, ('oct', 'box'))
The draws below stay inside these ranges and needn't reach their ends.
Inputs may be any that keep to these rules, and one draw needn't show every extreme that they name: `coarse_far_owner`: for a listing device with index d, the owner (d + 1) mod 128 appears exactly 8 times among that device's rows, and every other owner fewer times. `fine_far_owner`: for a listing device with index d, the owner (d + 1) mod 128 appears exactly 32 times among that device's rows, and every other owner fewer times. `coarse_near_shift`: the rows of each aligned block of 128 rows share one translation vector. `coarse_far_shift`: the rows of each aligned block of 128 rows share one translation vector. `fine_near_shift`: the rows of each aligned block of 128 rows share one translation vector. `fine_far_shift`: the rows of each aligned block of 128 rows share one translation vector.
All inputs are finite; a program needn't handle non-finite values.
Results may differ from the reference program's by a relative error of at most 0.0033.
Values may be sent and summed in bfloat16 or wider, within the bound.
No kernel may reach another device: no remote copies, remote signals or barrier semaphores. Data moves between devices by JAX's collectives and lax.ppermute only.
A program may use at most 128 MiB of HBM per device.

```python
import jax
import jax.numpy as jnp
from jax import lax

R = 64
NT = 316
BOX_C = 64
BOX_F = 512
NC = 8192
NF = 65536
NEAR_C = 1024
FAR_C = 512
NEAR_F = 8192
FAR_F = 2048
N_OCT = 4
N_BOX = 32
DEVICES = 128


def spread_owner(key, far_count):
    devices = N_OCT * N_BOX
    rows = jnp.arange(far_count, dtype=jnp.int32)
    capacity = 2 * far_count // devices
    first_key, second_key = jax.random.split(key)
    offset_start = jax.random.randint(first_key, (devices, 1), 0, devices - 1, dtype=jnp.int32)
    moves = jnp.where(rows[None, :] < capacity, 1, 2 + (rows[None, :] - capacity + offset_start) % (devices - 1)).astype(jnp.int32)
    scores = jax.random.randint(second_key, (devices, far_count), 0, 65536, dtype=jnp.int32) * far_count + rows[None, :]
    order = jnp.argsort(scores, axis=1, stable=True).astype(jnp.int32)
    moves = jnp.take_along_axis(moves, order, axis=1)
    device = jnp.arange(devices, dtype=jnp.int32)[:, None]
    owner = (device + moves) % devices
    return owner.astype(jnp.int32).reshape(devices * far_count, 1)


def grouped_shift(key, row_total):
    groups = row_total // 128
    kinds = jax.random.randint(key, (groups,), 0, NT, dtype=jnp.int32)
    marks = jnp.arange(groups, dtype=jnp.int32)
    kinds = jnp.where(marks == 0, NT - 1, jnp.where(marks == 1, 0, kinds)).astype(jnp.int32)
    return jnp.repeat(kinds, 128).astype(jnp.int32)


def draw_coarse_far_owner(key, part):
    key = jax.random.fold_in(key, 11)
    return spread_owner(key, FAR_C)


def draw_fine_far_owner(key, part):
    key = jax.random.fold_in(key, 23)
    return spread_owner(key, FAR_F)


def draw_coarse_near_shift(key, part):
    key = jax.random.fold_in(key, 31)
    return grouped_shift(key, NEAR_C * N_OCT * N_BOX)


def draw_coarse_far_shift(key, part):
    key = jax.random.fold_in(key, 37)
    return grouped_shift(key, FAR_C * N_OCT * N_BOX)


def draw_fine_near_shift(key, part):
    key = jax.random.fold_in(key, 41)
    return grouped_shift(key, NEAR_F * N_OCT * N_BOX)


def draw_fine_far_shift(key, part):
    key = jax.random.fold_in(key, 43)
    return grouped_shift(key, FAR_F * N_OCT * N_BOX)


def place_ends(result, rng, least, top_value):
    spot = [jax.random.randint(jax.random.fold_in(rng, axis), (), 0, length) for axis, length in enumerate(result.shape)]
    main_axis = result.shape.index(max(result.shape))
    neighbour = spot[:main_axis] + [(spot[main_axis] + 1) % result.shape[main_axis]] + spot[main_axis + 1:]
    return result.at[tuple(spot)].set(least).at[tuple(neighbour)].set(top_value)


def steps_of(stream_key, extent, shards, smallest, top_value):
    factor_of = 1.0
    for axis_at, blocks in shards:
        steps = jax.random.uniform(jax.random.fold_in(jax.random.fold_in(stream_key, 6), axis_at), (blocks,), jnp.float32, smallest / len(shards), top_value / len(shards))
        factor_of = factor_of * jnp.repeat(jnp.exp(steps), extent[axis_at] // blocks).reshape((-1,) + (1,) * (len(extent) - 1 - axis_at))
    return factor_of


def scatter_about(own_key, shape, scale, limit, pieces=(), held_as=jnp.bfloat16):
    factor_of = steps_of(own_key, shape, pieces, -0.22, 0.18) if pieces else 1.0
    array = jax.random.normal(own_key, shape, jnp.float32) * scale * factor_of
    return jnp.minimum(jnp.maximum(array, -limit), limit).astype(held_as)


def setup_inputs(seed: int = 0) -> dict:
    arg_keys = jax.random.split(jax.random.key(seed), 16)
    return {
        "coarse_multipole": scatter_about(arg_keys[0], (R, NC), 1.0, 6.0, ((1, 128),)),
        "fine_multipole": scatter_about(arg_keys[1], (R, NF), 1.0, 6.0, ((1, 128),)),
        "parent_local": scatter_about(arg_keys[2], (R, NC), 0.5, 4.0, ((1, 128),), jnp.float32),
        "operators": scatter_about(arg_keys[3], (NT, R, R), (64 * R) ** -0.5, 0.09375),
        "child_maps": scatter_about(arg_keys[4], (8, R, R), R ** -0.5, 0.75),
        "coarse_near_boxes": place_ends(jax.random.randint(arg_keys[5], (NEAR_C * DEVICES, 2), 0, BOX_C), jax.random.fold_in(arg_keys[5], 1), 0, BOX_C - 1).astype(jnp.int32),
        "coarse_near_shift": draw_coarse_near_shift(jax.random.fold_in(arg_keys[15], 71), 0),
        "coarse_far_boxes": place_ends(jax.random.randint(arg_keys[7], (FAR_C * DEVICES, 2), 0, BOX_C), jax.random.fold_in(arg_keys[7], 1), 0, BOX_C - 1).astype(jnp.int32),
        "coarse_far_owner": draw_coarse_far_owner(jax.random.fold_in(arg_keys[15], 71), 0),
        "coarse_far_shift": draw_coarse_far_shift(jax.random.fold_in(arg_keys[15], 71), 0),
        "fine_near_boxes": place_ends(jax.random.randint(arg_keys[10], (NEAR_F * DEVICES, 2), 0, BOX_F), jax.random.fold_in(arg_keys[10], 1), 0, BOX_F - 1).astype(jnp.int32),
        "fine_near_shift": draw_fine_near_shift(jax.random.fold_in(arg_keys[15], 71), 0),
        "fine_far_boxes": place_ends(jax.random.randint(arg_keys[12], (FAR_F * DEVICES, 2), 0, BOX_F), jax.random.fold_in(arg_keys[12], 1), 0, BOX_F - 1).astype(jnp.int32),
        "fine_far_owner": draw_fine_far_owner(jax.random.fold_in(arg_keys[15], 71), 0),
        "fine_far_shift": draw_fine_far_shift(jax.random.fold_in(arg_keys[15], 71), 0),
    }


def pair_products(operators, shift, vec_first, vec_second, scale):
    blocks = operators[shift].astype(jnp.float32)
    to_first = scale * jnp.einsum('bij,bj->bi', blocks, vec_second.astype(jnp.float32))
    to_second = scale * jnp.einsum('bji,bj->bi', blocks, vec_first.astype(jnp.float32))
    return to_first, to_second


def accumulate(totals, box_rows, operators, first_box, second_box, shift, per_device, scale):
    block_size = min(per_device, 1024)
    turns = first_box.shape[0] // block_size

    def step(index, running):
        start = index * block_size
        first_part = lax.dynamic_slice_in_dim(first_box, start, block_size)
        second_part = lax.dynamic_slice_in_dim(second_box, start, block_size)
        shift_part = lax.dynamic_slice_in_dim(shift, start, block_size)
        to_first, to_second = pair_products(operators, shift_part, box_rows[first_part], box_rows[second_part], scale)
        return running.at[first_part].add(to_first).at[second_part].add(to_second)

    return lax.fori_loop(0, turns, step, totals)


def level(totals, box_rows, operators, near_boxes, near_shift, far_boxes, far_owner, far_shift, box_count, near_count, far_count, scale):
    near_device = (jnp.arange(near_boxes.shape[0], dtype=jnp.int32) // near_count).astype(jnp.int32)
    near_first = (near_device * box_count + near_boxes[:, 0]).astype(jnp.int32)
    near_second = (near_device * box_count + near_boxes[:, 1]).astype(jnp.int32)
    totals = accumulate(totals, box_rows, operators, near_first, near_second, near_shift, near_count, scale)
    far_device = (jnp.arange(far_boxes.shape[0], dtype=jnp.int32) // far_count).astype(jnp.int32)
    far_first = (far_device * box_count + far_boxes[:, 0]).astype(jnp.int32)
    far_second = (far_owner[:, 0] * box_count + far_boxes[:, 1]).astype(jnp.int32)
    return accumulate(totals, box_rows, operators, far_first, far_second, far_shift, far_count, scale)


def reference(coarse_multipole, fine_multipole, parent_local, operators, child_maps, coarse_near_boxes, coarse_near_shift, coarse_far_boxes, coarse_far_owner, coarse_far_shift, fine_near_boxes, fine_near_shift, fine_far_boxes, fine_far_owner, fine_far_shift):
    totals = parent_local.T.astype(jnp.float32)
    totals = level(totals, coarse_multipole.T, operators, coarse_near_boxes, coarse_near_shift, coarse_far_boxes, coarse_far_owner, coarse_far_shift, BOX_C, NEAR_C, FAR_C, 1.0)
    coarse_local = totals.T.astype(jnp.bfloat16)
    fine_start = jnp.einsum('cij,jp->pci', child_maps.astype(jnp.float32), coarse_local.astype(jnp.float32)).reshape(NF, R)
    totals = level(fine_start, fine_multipole.T, operators, fine_near_boxes, fine_near_shift, fine_far_boxes, fine_far_owner, fine_far_shift, BOX_F, NEAR_F, FAR_F, 2.0)
    fine_local = totals.T.astype(jnp.bfloat16)
    return coarse_local, fine_local
```

```python
import jax
import jax.numpy as jnp
from jax import lax
from jax.experimental import pallas as pl
from jax.experimental.pallas import tpu as pltpu
from jax.sharding import PartitionSpec as P


F32 = jnp.float32
BF16 = jnp.bfloat16
I32 = jnp.int32

DEV = 128
RANK = 64
CAP_F = 32
CAP_C = 8
ROWS_F = CAP_F * RANK // 128
ROWS_C = CAP_C * RANK // 128
ROWS = 2 * (ROWS_F + ROWS_C)
HALF_CAP = CAP_F // 2
G_NEAR_F, G_FAR_F, G_NEAR_C, G_FAR_C = 64, 16, 8, 4
AT_FAR_F = G_NEAR_F
AT_NEAR_C = AT_FAR_F + G_FAR_F
AT_FAR_C = AT_NEAR_C + G_NEAR_C
GROUPS = 96
VMEM_LIMIT = 48 * 1024 * 1024


def mm(a, b):
    return lax.dot_general(a, b, (((1,), (0,)), ((), ())), preferred_element_type=F32)


def mm_nt(a, b):
    return lax.dot_general(a, b, (((1,), (1,)), ((), ())), preferred_element_type=F32)


def mm_tn(a, b):
    return lax.dot_general(a, b, (((0,), (0,)), ((), ())), preferred_element_type=F32)


def one_hot(row, count):
    n = row.shape[1]
    hit = lax.broadcasted_iota(I32, (count, n), 0) == row
    return jnp.where(hit, 1.0, 0.0).astype(BF16)


def half_stack(m):
    return jnp.concatenate([m[:, :256], m[:, 256:]], axis=0)


def pick_fine(stack, hot, row):
    both = mm(stack, hot)
    return jnp.where(row < 256, both[:RANK], both[RANK:])


def split_rows(values):
    high = values.astype(BF16)
    low = (values - high.astype(F32)).astype(BF16)
    return jnp.concatenate([high, low], axis=0)


def spread_fine(values, row):
    first = jnp.where(row < 256, values, 0.0)
    second = jnp.where(row < 256, 0.0, values)
    return split_rows(jnp.concatenate([first, second], axis=0))


def prefix_matrix():
    down = lax.broadcasted_iota(I32, (128, 256), 0)
    across = lax.broadcasted_iota(I32, (128, 256), 1)
    return jnp.where((down <= across) | (across >= 128), 1.0, 0.0).astype(BF16)


def route_kernel(f_owner, f_boxes, c_owner, c_boxes, slots_ref, f_pos, c_pos):
    prefix = prefix_matrix()

    def place(owner_ref, boxes_ref, pos_ref, blocks, cap, wide):
        carry = jnp.zeros((DEV, 128), F32)
        table = jnp.zeros((cap * (2 if wide else 1), DEV), F32)
        for b in range(blocks):
            lanes = slice(b * 128, (b + 1) * 128)
            hit = lax.broadcasted_iota(I32, (DEV, 128), 0) == owner_ref[:, lanes]
            hot = jnp.where(hit, 1.0, 0.0)
            counts = mm(hot.astype(BF16), prefix)
            seen = counts[:, :128] + carry
            pos = jnp.sum(jnp.where(hit, seen, 0.0), axis=0, keepdims=True) - 1.0
            carry = carry + counts[:, 128:]
            pos = pos.astype(I32)
            pos_ref[:, lanes] = pos
            slot = boxes_ref[1:2, lanes]
            here = lax.broadcasted_iota(I32, (cap, 128), 0) == pos
            low = jnp.where(here, (slot & 255).astype(F32), 0.0)
            if wide:
                high = jnp.where(here, (slot >> 8).astype(F32), 0.0)
                low = jnp.concatenate([low, high], axis=0)
            table = table + mm_nt(low.astype(BF16), hot.astype(BF16))
        if wide:
            table = table[:cap] + 256.0 * table[cap:]
        return table

    fine = place(f_owner, f_boxes, f_pos, 16, CAP_F, True)
    coarse = place(c_owner, c_boxes, c_pos, 4, CAP_C, False)
    rest = jnp.zeros((128 - CAP_F - CAP_C, DEV), F32)
    table = jnp.concatenate([fine, coarse, rest], axis=0)
    slots_ref[:, 0, :] = jnp.transpose(table).astype(I32)


def outgoing_kernel(
    ops, s_nf, s_ff, s_nc, s_fc, fm, cm, f_owner, f_boxes, f_pos, c_owner, c_boxes, c_pos,
    sel_ref, part_ref, kinds, kf, pm, hot_out, pm_c, flat,
):
    kinds[...] = jnp.zeros_like(kinds)
    kinds[0:AT_FAR_F] = s_nf[...]
    kinds[AT_FAR_F:AT_NEAR_C] = s_ff[...]
    kinds[AT_NEAR_C:AT_FAR_C] = s_nc[...]
    kinds[AT_FAR_C:AT_FAR_C + G_FAR_C] = s_fc[...]
    nt = ops.shape[2]
    hot_kind = jnp.where(
        kinds[:, 0:1] == lax.broadcasted_iota(I32, (GROUPS, nt), 1), 1.0, 0.0
    ).astype(BF16)
    for quad in range(RANK // 4):
        rows = ops[quad * 4:(quad + 1) * 4].reshape(256, nt)
        got = mm_nt(hot_kind, rows)
        for k in range(4):
            kf[pl.ds(quad * 4 + k, GROUPS, stride=RANK), :] = got[:, k * RANK:(k + 1) * RANK]
    sel_ref[...] = kf[...].reshape(GROUPS, RANK, RANK).astype(BF16)

    stack = half_stack(fm[...])
    for g in range(G_FAR_F):
        lanes = slice(g * 128, (g + 1) * 128)
        row = f_boxes[0:1, lanes]
        vec = pick_fine(stack, one_hot(row & 255, 256), row).astype(BF16)
        part = 2.0 * mm_tn(sel_ref[AT_FAR_F + g], vec)
        pos = f_pos[:, lanes]
        hot_out[:, lanes] = one_hot((pos >> 4) * DEV + f_owner[:, lanes], 2 * DEV)
        step = pos & (HALF_CAP - 1)
        for k in range(HALF_CAP):
            pm[k * RANK:(k + 1) * RANK, lanes] = jnp.where(step == k, part, 0.0).astype(BF16)
    for kp in range(HALF_CAP // 2):
        block = mm_nt(pm[kp * 128:(kp + 1) * 128, :], hot_out[...])
        for half in range(2):
            turned = jnp.transpose(block[:, half * DEV:(half + 1) * DEV])
            flat[pl.ds(half * (HALF_CAP // 2) + kp, DEV, stride=ROWS // 2), :] = turned

    hot_list = []
    for g in range(G_FAR_C):
        lanes = slice(g * 128, (g + 1) * 128)
        vec = mm(cm[...], one_hot(c_boxes[0:1, lanes], 64)).astype(BF16)
        part = mm_tn(sel_ref[AT_FAR_C + g], vec)
        pos = c_pos[:, lanes]
        hot_list.append(one_hot(c_owner[:, lanes], DEV))
        for k in range(CAP_C):
            pm_c[k * RANK:(k + 1) * RANK, lanes] = jnp.where(pos == k, part, 0.0).astype(BF16)
    hot_c = jnp.concatenate(hot_list, axis=1)
    for kp in range(CAP_C // 2):
        block = mm_nt(pm_c[kp * 128:(kp + 1) * 128, :], hot_c)
        flat[pl.ds(ROWS_F + kp, DEV, stride=ROWS // 2), :] = jnp.transpose(block)
    part_ref[...] = flat[...].reshape(DEV, ROWS // 2, 128).astype(BF16)


def reply_kernel(slots, fm, cm, part, out_ref, flat):
    table = jnp.transpose(slots[:, 0, :].astype(F32)).astype(I32)
    stack = half_stack(fm[...])
    for kp in range(ROWS_F):
        row = jnp.concatenate([table[2 * kp:2 * kp + 1], table[2 * kp + 1:2 * kp + 2]], axis=1)
        vec = pick_fine(stack, one_hot(row & 255, 256), row)
        both = jnp.concatenate([vec[:, :DEV], vec[:, DEV:]], axis=0)
        flat[pl.ds(kp, DEV, stride=ROWS // 2), :] = jnp.transpose(both)
    for kp in range(ROWS_C):
        at = CAP_F + 2 * kp
        row = jnp.concatenate([table[at:at + 1], table[at + 1:at + 2]], axis=1)
        vec = mm(cm[...], one_hot(row, 64))
        both = jnp.concatenate([vec[:, :DEV], vec[:, DEV:]], axis=0)
        flat[pl.ds(ROWS_F + kp, DEV, stride=ROWS // 2), :] = jnp.transpose(both)
    replies = flat[...].reshape(DEV, ROWS // 2, 128)
    out_ref[...] = jnp.concatenate([replies, part[...].astype(F32)], axis=1).astype(BF16)


def near_kernel(sel, fm, cm, f_boxes, c_boxes, f_out, c_out):
    stack = half_stack(fm[...])
    f_out[...] = jnp.zeros_like(f_out)

    def step(i, carry):
        lanes = pl.ds(pl.multiple_of(i * 256, 256), 256)
        first = f_boxes[0:1, lanes]
        second = f_boxes[1:2, lanes]
        hot_1 = one_hot(first & 255, 256)
        hot_2 = one_hot(second & 255, 256)
        vec_1 = pick_fine(stack, hot_1, first).astype(BF16)
        vec_2 = pick_fine(stack, hot_2, second).astype(BF16)
        to_1, to_2 = [], []
        for k in range(2):
            op = sel[2 * i + k]
            cut = slice(k * 128, (k + 1) * 128)
            to_1.append(mm(op, vec_2[:, cut]))
            to_2.append(mm_tn(op, vec_1[:, cut]))
        to_1 = jnp.concatenate(to_1, axis=1)
        to_2 = jnp.concatenate(to_2, axis=1)
        f_out[...] += mm_nt(spread_fine(to_1, first), hot_1) + mm_nt(
            spread_fine(to_2, second), hot_2
        )
        return carry

    lax.fori_loop(0, G_NEAR_F // 2, step, 0)
    total = jnp.zeros((2 * RANK, 64), F32)
    for g in range(G_NEAR_C):
        lanes = slice(g * 128, (g + 1) * 128)
        hot_1 = one_hot(c_boxes[0:1, lanes], 64)
        hot_2 = one_hot(c_boxes[1:2, lanes], 64)
        vec_1 = mm(cm[...], hot_1).astype(BF16)
        vec_2 = mm(cm[...], hot_2).astype(BF16)
        op = sel[AT_NEAR_C + g]
        total = total + mm_nt(split_rows(mm(op, vec_2)), hot_1)
        total = total + mm_nt(split_rows(mm_tn(op, vec_1)), hot_2)
    c_out[...] = total


def final_kernel(
    got, slots, sel, f_near, c_near, parent, maps, f_owner, f_boxes, f_pos, c_owner, c_boxes, c_pos,
    c_ref, f_ref, flat, held, turned_c,
):
    flat[...] = got[...].astype(F32).reshape(DEV * ROWS, 128)
    table = jnp.transpose(slots[:, 0, :].astype(F32)).astype(I32)

    def turned(row):
        return jnp.transpose(flat[pl.ds(row, DEV, stride=ROWS), :])

    for kp in range(ROWS_C):
        turned_c[kp * 128:(kp + 1) * 128, :] = turned(ROWS_F + kp).astype(BF16)
    total_c = c_near[...]
    for g in range(G_FAR_C):
        lanes = slice(g * 128, (g + 1) * 128)
        found = mm(turned_c[...], one_hot(c_owner[:, lanes], DEV))
        pos = c_pos[:, lanes]
        vec = jnp.zeros((RANK, 128), F32)
        for k in range(CAP_C):
            vec = jnp.where(pos == k, found[k * RANK:(k + 1) * RANK], vec)
        to_1 = mm(sel[AT_FAR_C + g], vec.astype(BF16))
        total_c = total_c + mm_nt(split_rows(to_1), one_hot(c_boxes[0:1, lanes], 64))
    for kp in range(ROWS_C):
        arrived = turned(ROWS // 2 + ROWS_F + kp).astype(BF16)
        for par in range(2):
            at = CAP_F + 2 * kp + par
            add = mm_nt(arrived[par * RANK:(par + 1) * RANK], one_hot(table[at:at + 1], 64))
            total_c = total_c + jnp.concatenate([add, jnp.zeros_like(add)], axis=0)
    coarse = (parent[...] + total_c[:RANK] + total_c[RANK:]).astype(BF16)
    c_ref[...] = coarse

    box = lax.broadcasted_iota(I32, (64, 512), 1)
    parent_of = jnp.where((box >> 3) == lax.broadcasted_iota(I32, (64, 512), 0), 1.0, 0.0)
    wide = mm(coarse, parent_of.astype(BF16)).astype(BF16)
    start = jnp.zeros((RANK, 512), F32)
    for k in range(8):
        start = jnp.where((box & 7) == k, mm(maps[k], wide), start)

    for half in range(2):
        for kp in range(HALF_CAP // 2):
            held[kp * 128:(kp + 1) * 128, half * DEV:(half + 1) * DEV] = turned(
                half * (HALF_CAP // 2) + kp
            ).astype(BF16)
    total = f_near[...]
    for i in range(G_FAR_F // 2):
        lanes = slice(i * 256, (i + 1) * 256)
        pos = f_pos[:, lanes]
        found = mm(held[...], one_hot((pos >> 4) * DEV + f_owner[:, lanes], 2 * DEV))
        where = pos & (HALF_CAP - 1)
        vec = jnp.zeros((RANK, 256), F32)
        for k in range(HALF_CAP):
            vec = jnp.where(where == k, found[k * RANK:(k + 1) * RANK], vec)
        vec = vec.astype(BF16)
        to_1 = jnp.concatenate(
            [mm(sel[AT_FAR_F + 2 * i + k], vec[:, k * 128:(k + 1) * 128]) for k in range(2)], axis=1
        )
        first = f_boxes[0:1, lanes]
        total = total + mm_nt(spread_fine(to_1, first), one_hot(first & 255, 256))
    added = jnp.zeros((2 * RANK, 256), F32)
    for kp in range(ROWS_F):
        arrived = turned(ROWS // 2 + kp)
        row = jnp.concatenate([table[2 * kp:2 * kp + 1], table[2 * kp + 1:2 * kp + 2]], axis=1)
        side = jnp.concatenate([arrived[:RANK], arrived[RANK:]], axis=1)
        both = jnp.concatenate(
            [jnp.where(row < 256, side, 0.0), jnp.where(row < 256, 0.0, side)], axis=0
        )
        added = added + mm_nt(both.astype(BF16), one_hot(row & 255, 256))
    total = 2.0 * (total[:2 * RANK] + total[2 * RANK:]) + added
    fine = start + jnp.concatenate([total[:RANK], total[RANK:]], axis=1)
    f_ref[...] = fine.astype(BF16)


def call(kernel, out_shape, scratch, flops, nbytes, *args):
    return pl.pallas_call(
        kernel,
        out_shape=out_shape,
        scratch_shapes=scratch,
        compiler_params=pltpu.CompilerParams(vmem_limit_bytes=VMEM_LIMIT),
        cost_estimate=pl.CostEstimate(flops=flops, bytes_accessed=nbytes, transcendentals=0),
    )(*args)


def on_device(
    coarse_multipole,
    fine_multipole,
    parent_local,
    operators,
    child_maps,
    coarse_near_boxes,
    coarse_near_shift,
    coarse_far_boxes,
    coarse_far_owner,
    coarse_far_shift,
    fine_near_boxes,
    fine_near_shift,
    fine_far_boxes,
    fine_far_owner,
    fine_far_shift,
):
    def sds(shape, dtype):
        return jax.ShapeDtypeStruct(shape, dtype)

    fm, cm = fine_multipole, coarse_multipole
    f_owner, c_owner = fine_far_owner.T, coarse_far_owner.T
    f_far, c_far = fine_far_boxes.T, coarse_far_boxes.T
    ops = jnp.transpose(operators, (1, 2, 0))

    slots, f_pos, c_pos = call(
        route_kernel,
        (sds((DEV, 1, 128), I32), sds((1, 2048), I32), sds((1, 512), I32)),
        [],
        10**9,
        10**6,
        f_owner, f_far, c_owner, c_far,
    )
    asked = lax.all_to_all(slots, ("oct", "box"), split_axis=0, concat_axis=0, tiled=True)
    sel, part = call(
        outgoing_kernel,
        (sds((GROUPS, RANK, RANK), BF16), sds((DEV, ROWS // 2, 128), BF16)),
        [
            pltpu.VMEM((GROUPS, 128), I32),
            pltpu.VMEM((GROUPS * RANK, RANK), F32),
            pltpu.VMEM((HALF_CAP * RANK, 2048), BF16),
            pltpu.VMEM((2 * DEV, 2048), BF16),
            pltpu.VMEM((CAP_C * RANK, 512), BF16),
            pltpu.VMEM((DEV * ROWS // 2, 128), F32),
        ],
        5 * 10**9,
        10**7,
        ops,
        fine_near_shift.reshape(-1, 128),
        fine_far_shift.reshape(-1, 128),
        coarse_near_shift.reshape(-1, 128),
        coarse_far_shift.reshape(-1, 128),
        fm, cm, f_owner, f_far, f_pos, c_owner, c_far, c_pos,
    )
    sent = call(
        reply_kernel,
        sds((DEV, ROWS, 128), BF16),
        [pltpu.VMEM((DEV * ROWS // 2, 128), F32)],
        10**9,
        10**6,
        asked, fm, cm, part,
    )
    got = lax.all_to_all(sent, ("oct", "box"), split_axis=0, concat_axis=0, tiled=True)
    f_near, c_near = call(
        near_kernel,
        (sds((4 * RANK, 256), F32), sds((2 * RANK, 64), F32)),
        [],
        10**10,
        10**7,
        sel, fm, cm, fine_near_boxes.T, coarse_near_boxes.T,
    )
    return call(
        final_kernel,
        (sds((RANK, 64), BF16), sds((RANK, 512), BF16)),
        [
            pltpu.VMEM((DEV * ROWS, 128), F32),
            pltpu.VMEM((HALF_CAP * RANK, 2 * DEV), BF16),
            pltpu.VMEM((CAP_C * RANK, DEV), BF16),
        ],
        3 * 10**9,
        10**7,
        got, asked, sel, f_near, c_near, parent_local, child_maps,
        f_owner, f_far, f_pos, c_owner, c_far, c_pos,
    )


def solution(mesh):
    both = ("oct", "box")
    return jax.shard_map(
        on_device,
        mesh=mesh,
        in_specs=(
            P(None, both),
            P(None, both),
            P(None, both),
            P(),
            P(),
            P(both, None),
            P(both),
            P(both, None),
            P(both, None),
            P(both),
            P(both, None),
            P(both),
            P(both, None),
            P(both, None),
            P(both),
        ),
        out_specs=(P(None, both), P(None, both)),
        check_vma=False,
    )
```

```python
import jax
import jax.numpy as jnp
from jax import lax
from jax.experimental import pallas as pl
from jax.experimental.pallas import tpu as pltpu
from jax.sharding import PartitionSpec as P


F32 = jnp.float32
BF16 = jnp.bfloat16
I32 = jnp.int32

DEV = 128
RANK = 64
CAP_F = 32
CAP_C = 8
ROWS_F = CAP_F * RANK // 128
ROWS_C = CAP_C * RANK // 128
ROWS = 2 * (ROWS_F + ROWS_C)
HALF_CAP = CAP_F // 2
G_NEAR_F, G_FAR_F, G_NEAR_C, G_FAR_C = 64, 16, 8, 4
AT_FAR_F = G_NEAR_F
AT_NEAR_C = AT_FAR_F + G_FAR_F
AT_FAR_C = AT_NEAR_C + G_NEAR_C
GROUPS = 96
NEAR_BLOCK = 4096
FAR_BLOCK = 2048
PM_ROWS = 512
VMEM_LIMIT = 48 * 1024 * 1024


def mm(a, b):
    return lax.dot_general(a, b, (((1,), (0,)), ((), ())), preferred_element_type=F32)


def mm_nt(a, b):
    return lax.dot_general(a, b, (((1,), (1,)), ((), ())), preferred_element_type=F32)


def mm_tn(a, b):
    return lax.dot_general(a, b, (((0,), (0,)), ((), ())), preferred_element_type=F32)


def one_hot(row, count):
    n = row.shape[1]
    at = lax.broadcasted_iota(I32, (count, n), 0).astype(BF16)
    hit = at == jnp.broadcast_to(row.astype(BF16), (count, n))
    return jnp.where(hit, jnp.ones((), BF16), jnp.zeros((), BF16))


def half_stack(m):
    return jnp.concatenate([m[:, :256], m[:, 256:]], axis=0)


def pick_fine(stack, hot, row):
    both = mm(stack, hot)
    return jnp.where(row < 256, both[:RANK], both[RANK:])


def split_rows(values):
    high = values.astype(BF16)
    low = (values - high.astype(F32)).astype(BF16)
    return jnp.concatenate([high, low], axis=0)


def spread_fine(values, row):
    first = jnp.where(row < 256, values, 0.0)
    second = jnp.where(row < 256, 0.0, values)
    return split_rows(jnp.concatenate([first, second], axis=0))


def prefix_matrix():
    down = lax.broadcasted_iota(I32, (128, 256), 0)
    across = lax.broadcasted_iota(I32, (128, 256), 1)
    return jnp.where((down <= across) | (across >= 128), 1.0, 0.0).astype(BF16)


def route_kernel(f_owner, f_boxes, c_owner, c_boxes, slots_ref, f_pos, c_pos):
    prefix = prefix_matrix()

    def place(owner_ref, boxes_ref, pos_ref, blocks, cap, wide):
        carry = jnp.zeros((DEV, 128), F32)
        table = jnp.zeros((cap * (2 if wide else 1), DEV), F32)
        for b in range(blocks):
            lanes = slice(b * 128, (b + 1) * 128)
            hit = lax.broadcasted_iota(I32, (DEV, 128), 0) == owner_ref[:, lanes]
            hot = jnp.where(hit, 1.0, 0.0)
            counts = mm(hot.astype(BF16), prefix)
            seen = counts[:, :128] + carry
            pos = jnp.sum(jnp.where(hit, seen, 0.0), axis=0, keepdims=True) - 1.0
            carry = carry + counts[:, 128:]
            pos = pos.astype(I32)
            pos_ref[:, lanes] = pos
            slot = boxes_ref[1:2, lanes]
            here = lax.broadcasted_iota(I32, (cap, 128), 0) == pos
            low = jnp.where(here, (slot & 255).astype(F32), 0.0)
            if wide:
                high = jnp.where(here, (slot >> 8).astype(F32), 0.0)
                low = jnp.concatenate([low, high], axis=0)
            table = table + mm_nt(low.astype(BF16), hot.astype(BF16))
        if wide:
            table = table[:cap] + 256.0 * table[cap:]
        return table

    fine = place(f_owner, f_boxes, f_pos, 16, CAP_F, True)
    coarse = place(c_owner, c_boxes, c_pos, 4, CAP_C, False)
    rest = jnp.zeros((128 - CAP_F - CAP_C, DEV), F32)
    table = jnp.concatenate([fine, coarse, rest], axis=0)
    slots_ref[:, 0, :] = jnp.transpose(table).astype(I32)


def outgoing_kernel(
    ops, s_nf, s_ff, s_nc, s_fc, fm, cm, f_owner, f_boxes, f_pos, c_owner, c_boxes, c_pos,
    sel_ref, part_ref, kinds, kf, pm, hot_out, pm_c, flat,
):
    kinds[...] = jnp.zeros_like(kinds)
    kinds[0:AT_FAR_F] = s_nf[...]
    kinds[AT_FAR_F:AT_NEAR_C] = s_ff[...]
    kinds[AT_NEAR_C:AT_FAR_C] = s_nc[...]
    kinds[AT_FAR_C:AT_FAR_C + G_FAR_C] = s_fc[...]
    nt = ops.shape[2]
    hot_kind = jnp.where(
        kinds[:, 0:1] == lax.broadcasted_iota(I32, (GROUPS, nt), 1), 1.0, 0.0
    ).astype(BF16)
    for quad in range(RANK // 4):
        rows = ops[quad * 4:(quad + 1) * 4].reshape(256, nt)
        got = mm_nt(hot_kind, rows)
        for k in range(4):
            kf[pl.ds(quad * 4 + k, GROUPS, stride=RANK), :] = got[:, k * RANK:(k + 1) * RANK]
    sel_ref[...] = kf[...].reshape(GROUPS, RANK, RANK).astype(BF16)

    stack = half_stack(fm[...])
    row = f_boxes[0:1, :]
    vec = pick_fine(stack, one_hot(row & 255, 256), row).astype(BF16)
    part = jnp.concatenate(
        [
            mm_tn(sel_ref[AT_FAR_F + g], vec[:, g * 128:(g + 1) * 128])
            for g in range(G_FAR_F)
        ],
        axis=1,
    )
    part = (2.0 * part).astype(BF16)
    pos = f_pos[...]
    hot_out[...] = one_hot((pos >> 4) * DEV + f_owner[...], 2 * DEV)
    step = jnp.broadcast_to((pos & (HALF_CAP - 1)).astype(BF16), part.shape)
    none = jnp.zeros((), BF16)
    for k in range(HALF_CAP):
        pm[k * RANK:(k + 1) * RANK, :] = jnp.where(step == jnp.asarray(k, BF16), part, none)
    for j in range(HALF_CAP * RANK // PM_ROWS):
        big = mm_nt(pm[j * PM_ROWS:(j + 1) * PM_ROWS, :], hot_out[...])
        for i in range(PM_ROWS // 128):
            kp = j * (PM_ROWS // 128) + i
            for half in range(2):
                turned = jnp.transpose(big[i * 128:(i + 1) * 128, half * DEV:(half + 1) * DEV])
                flat[pl.ds(half * (HALF_CAP // 2) + kp, DEV, stride=ROWS // 2), :] = turned

    hot_list = []
    for g in range(G_FAR_C):
        lanes = slice(g * 128, (g + 1) * 128)
        vec = mm(cm[...], one_hot(c_boxes[0:1, lanes], 64)).astype(BF16)
        part = mm_tn(sel_ref[AT_FAR_C + g], vec)
        pos = c_pos[:, lanes]
        hot_list.append(one_hot(c_owner[:, lanes], DEV))
        for k in range(CAP_C):
            pm_c[k * RANK:(k + 1) * RANK, lanes] = jnp.where(pos == k, part, 0.0).astype(BF16)
    hot_c = jnp.concatenate(hot_list, axis=1)
    for kp in range(CAP_C // 2):
        block = mm_nt(pm_c[kp * 128:(kp + 1) * 128, :], hot_c)
        flat[pl.ds(ROWS_F + kp, DEV, stride=ROWS // 2), :] = jnp.transpose(block)
    part_ref[...] = flat[...].reshape(DEV, ROWS // 2, 128).astype(BF16)


def reply_kernel(slots, fm, cm, part, out_ref, flat):
    table = jnp.transpose(slots[:, 0, :].astype(F32)).astype(I32)
    stack = half_stack(fm[...])
    for kp in range(ROWS_F):
        row = jnp.concatenate([table[2 * kp:2 * kp + 1], table[2 * kp + 1:2 * kp + 2]], axis=1)
        vec = pick_fine(stack, one_hot(row & 255, 256), row)
        both = jnp.concatenate([vec[:, :DEV], vec[:, DEV:]], axis=0)
        flat[pl.ds(kp, DEV, stride=ROWS // 2), :] = jnp.transpose(both)
    for kp in range(ROWS_C):
        at = CAP_F + 2 * kp
        row = jnp.concatenate([table[at:at + 1], table[at + 1:at + 2]], axis=1)
        vec = mm(cm[...], one_hot(row, 64))
        both = jnp.concatenate([vec[:, :DEV], vec[:, DEV:]], axis=0)
        flat[pl.ds(ROWS_F + kp, DEV, stride=ROWS // 2), :] = jnp.transpose(both)
    replies = flat[...].reshape(DEV, ROWS // 2, 128)
    out_ref[...] = jnp.concatenate([replies, part[...].astype(F32)], axis=1).astype(BF16)


def near_kernel(sel, fm, cm, f_boxes, c_boxes, f_out, c_out):
    stack = half_stack(fm[...])
    f_out[...] = jnp.zeros_like(f_out)

    def step(i, carry):
        lanes = pl.ds(pl.multiple_of(i * NEAR_BLOCK, NEAR_BLOCK), NEAR_BLOCK)
        first = f_boxes[0:1, lanes]
        second = f_boxes[1:2, lanes]
        hot_1 = one_hot(first & 255, 256)
        hot_2 = one_hot(second & 255, 256)
        vec_1 = pick_fine(stack, hot_1, first).astype(BF16)
        vec_2 = pick_fine(stack, hot_2, second).astype(BF16)
        to_1, to_2 = [], []
        for k in range(NEAR_BLOCK // 128):
            op = sel[NEAR_BLOCK // 128 * i + k]
            cut = slice(k * 128, (k + 1) * 128)
            to_1.append(mm(op, vec_2[:, cut]))
            to_2.append(mm_tn(op, vec_1[:, cut]))
        to_1 = jnp.concatenate(to_1, axis=1)
        to_2 = jnp.concatenate(to_2, axis=1)
        both = jnp.concatenate([spread_fine(to_1, first), spread_fine(to_2, second)], axis=1)
        hots = jnp.concatenate([hot_1, hot_2], axis=1)
        f_out[...] += mm_nt(both, hots)
        return carry

    lax.fori_loop(0, G_NEAR_F * 128 // NEAR_BLOCK, step, 0)
    total = jnp.zeros((2 * RANK, 64), F32)
    for g in range(G_NEAR_C):
        lanes = slice(g * 128, (g + 1) * 128)
        hot_1 = one_hot(c_boxes[0:1, lanes], 64)
        hot_2 = one_hot(c_boxes[1:2, lanes], 64)
        vec_1 = mm(cm[...], hot_1).astype(BF16)
        vec_2 = mm(cm[...], hot_2).astype(BF16)
        op = sel[AT_NEAR_C + g]
        total = total + mm_nt(split_rows(mm(op, vec_2)), hot_1)
        total = total + mm_nt(split_rows(mm_tn(op, vec_1)), hot_2)
    c_out[...] = total


def final_kernel(
    got, slots, sel, f_near, c_near, parent, maps, f_owner, f_boxes, f_pos, c_owner, c_boxes, c_pos,
    c_ref, f_ref, flat, held, turned_c,
):
    flat[...] = got[...].astype(F32).reshape(DEV * ROWS, 128)
    table = jnp.transpose(slots[:, 0, :].astype(F32)).astype(I32)

    def turned(row):
        return jnp.transpose(flat[pl.ds(row, DEV, stride=ROWS), :])

    for kp in range(ROWS_C):
        turned_c[kp * 128:(kp + 1) * 128, :] = turned(ROWS_F + kp).astype(BF16)
    total_c = c_near[...]
    for g in range(G_FAR_C):
        lanes = slice(g * 128, (g + 1) * 128)
        found = mm(turned_c[...], one_hot(c_owner[:, lanes], DEV))
        pos = c_pos[:, lanes]
        vec = jnp.zeros((RANK, 128), F32)
        for k in range(CAP_C):
            vec = jnp.where(pos == k, found[k * RANK:(k + 1) * RANK], vec)
        to_1 = mm(sel[AT_FAR_C + g], vec.astype(BF16))
        total_c = total_c + mm_nt(split_rows(to_1), one_hot(c_boxes[0:1, lanes], 64))
    for kp in range(ROWS_C):
        arrived = turned(ROWS // 2 + ROWS_F + kp).astype(BF16)
        for par in range(2):
            at = CAP_F + 2 * kp + par
            add = mm_nt(arrived[par * RANK:(par + 1) * RANK], one_hot(table[at:at + 1], 64))
            total_c = total_c + jnp.concatenate([add, jnp.zeros_like(add)], axis=0)
    coarse = (parent[...] + total_c[:RANK] + total_c[RANK:]).astype(BF16)
    c_ref[...] = coarse

    box = lax.broadcasted_iota(I32, (64, 512), 1)
    parent_of = jnp.where((box >> 3) == lax.broadcasted_iota(I32, (64, 512), 0), 1.0, 0.0)
    wide = mm(coarse, parent_of.astype(BF16)).astype(BF16)
    start = jnp.zeros((RANK, 512), F32)
    for k in range(8):
        start = jnp.where((box & 7) == k, mm(maps[k], wide), start)

    for half in range(2):
        for kp in range(HALF_CAP // 2):
            held[kp * 128:(kp + 1) * 128, half * DEV:(half + 1) * DEV] = turned(
                half * (HALF_CAP // 2) + kp
            ).astype(BF16)
    total = f_near[...]
    for i in range(2048 // FAR_BLOCK):
        lanes = slice(i * FAR_BLOCK, (i + 1) * FAR_BLOCK)
        pos = f_pos[:, lanes]
        found = mm(held[...], one_hot((pos >> 4) * DEV + f_owner[:, lanes], 2 * DEV))
        where = pos & (HALF_CAP - 1)
        vec = jnp.zeros((RANK, FAR_BLOCK), F32)
        for k in range(HALF_CAP):
            vec = jnp.where(where == k, found[k * RANK:(k + 1) * RANK], vec)
        vec = vec.astype(BF16)
        each = FAR_BLOCK // 128
        to_1 = jnp.concatenate(
            [mm(sel[AT_FAR_F + each * i + k], vec[:, k * 128:(k + 1) * 128]) for k in range(each)],
            axis=1,
        )
        first = f_boxes[0:1, lanes]
        total = total + mm_nt(spread_fine(to_1, first), one_hot(first & 255, 256))
    sides, hots = [], []
    for kp in range(ROWS_F):
        arrived = turned(ROWS // 2 + kp)
        row = jnp.concatenate([table[2 * kp:2 * kp + 1], table[2 * kp + 1:2 * kp + 2]], axis=1)
        side = jnp.concatenate([arrived[:RANK], arrived[RANK:]], axis=1)
        none = jnp.zeros((), BF16)
        upper = jnp.broadcast_to(row, side.shape) < 256
        sides.append(
            jnp.concatenate([jnp.where(upper, side, 0.0), jnp.where(upper, 0.0, side)], axis=0).astype(BF16)
        )
        hots.append(one_hot(row & 255, 256))
    added = mm_nt(jnp.concatenate(sides, axis=1), jnp.concatenate(hots, axis=1))
    total = 2.0 * (total[:2 * RANK] + total[2 * RANK:]) + added
    fine = start + jnp.concatenate([total[:RANK], total[RANK:]], axis=1)
    f_ref[...] = fine.astype(BF16)


def call(kernel, out_shape, scratch, flops, nbytes, *args):
    return pl.pallas_call(
        kernel,
        out_shape=out_shape,
        scratch_shapes=scratch,
        compiler_params=pltpu.CompilerParams(vmem_limit_bytes=VMEM_LIMIT),
        cost_estimate=pl.CostEstimate(flops=flops, bytes_accessed=nbytes, transcendentals=0),
    )(*args)


def on_device(
    coarse_multipole,
    fine_multipole,
    parent_local,
    operators,
    child_maps,
    coarse_near_boxes,
    coarse_near_shift,
    coarse_far_boxes,
    coarse_far_owner,
    coarse_far_shift,
    fine_near_boxes,
    fine_near_shift,
    fine_far_boxes,
    fine_far_owner,
    fine_far_shift,
):
    def sds(shape, dtype):
        return jax.ShapeDtypeStruct(shape, dtype)

    fm, cm = fine_multipole, coarse_multipole
    f_owner, c_owner = fine_far_owner.T, coarse_far_owner.T
    f_far, c_far = fine_far_boxes.T, coarse_far_boxes.T
    ops = jnp.transpose(operators, (1, 2, 0))

    slots, f_pos, c_pos = call(
        route_kernel,
        (sds((DEV, 1, 128), I32), sds((1, 2048), I32), sds((1, 512), I32)),
        [],
        10**9,
        10**6,
        f_owner, f_far, c_owner, c_far,
    )
    asked = lax.all_to_all(slots, ("oct", "box"), split_axis=0, concat_axis=0, tiled=True)
    sel, part = call(
        outgoing_kernel,
        (sds((GROUPS, RANK, RANK), BF16), sds((DEV, ROWS // 2, 128), BF16)),
        [
            pltpu.VMEM((GROUPS, 128), I32),
            pltpu.VMEM((GROUPS * RANK, RANK), F32),
            pltpu.VMEM((HALF_CAP * RANK, 2048), BF16),
            pltpu.VMEM((2 * DEV, 2048), BF16),
            pltpu.VMEM((CAP_C * RANK, 512), BF16),
            pltpu.VMEM((DEV * ROWS // 2, 128), F32),
        ],
        5 * 10**9,
        10**7,
        ops,
        fine_near_shift.reshape(-1, 128),
        fine_far_shift.reshape(-1, 128),
        coarse_near_shift.reshape(-1, 128),
        coarse_far_shift.reshape(-1, 128),
        fm, cm, f_owner, f_far, f_pos, c_owner, c_far, c_pos,
    )
    sent = call(
        reply_kernel,
        sds((DEV, ROWS, 128), BF16),
        [pltpu.VMEM((DEV * ROWS // 2, 128), F32)],
        10**9,
        10**6,
        asked, fm, cm, part,
    )
    got = lax.all_to_all(sent, ("oct", "box"), split_axis=0, concat_axis=0, tiled=True)
    f_near, c_near = call(
        near_kernel,
        (sds((4 * RANK, 256), F32), sds((2 * RANK, 64), F32)),
        [],
        10**10,
        10**7,
        sel, fm, cm, fine_near_boxes.T, coarse_near_boxes.T,
    )
    return call(
        final_kernel,
        (sds((RANK, 64), BF16), sds((RANK, 512), BF16)),
        [
            pltpu.VMEM((DEV * ROWS, 128), F32),
            pltpu.VMEM((HALF_CAP * RANK, 2 * DEV), BF16),
            pltpu.VMEM((CAP_C * RANK, DEV), BF16),
        ],
        3 * 10**9,
        10**7,
        got, asked, sel, f_near, c_near, parent_local, child_maps,
        f_owner, f_far, f_pos, c_owner, c_far, c_pos,
    )


def solution(mesh):
    both = ("oct", "box")
    return jax.shard_map(
        on_device,
        mesh=mesh,
        in_specs=(
            P(None, both),
            P(None, both),
            P(None, both),
            P(),
            P(),
            P(both, None),
            P(both),
            P(both, None),
            P(both, None),
            P(both),
            P(both, None),
            P(both),
            P(both, None),
            P(both, None),
            P(both),
        ),
        out_specs=(P(None, both), P(None, both)),
        check_vma=False,
    )
```

```python
import jax
import jax.numpy as jnp
from jax import lax
from jax.experimental import pallas as pl
from jax.experimental.pallas import tpu as pltpu
from jax.sharding import PartitionSpec as P


F32 = jnp.float32
BF16 = jnp.bfloat16
I32 = jnp.int32

DEV = 128
RANK = 64
CAP_F = 32
CAP_C = 8
ROWS_F = CAP_F * RANK // 128
ROWS_C = CAP_C * RANK // 128
ROWS = 2 * (ROWS_F + ROWS_C)
HALF_CAP = CAP_F // 2
PART_CAP = CAP_F // 4
G_NEAR_F, G_FAR_F, G_NEAR_C, G_FAR_C = 64, 16, 8, 4
FAR_GROUPS = 24
NEAR_GROUPS = G_NEAR_F + G_NEAR_C
NEAR_BLOCK = 4096
PM_ROWS = 512
MIB_1, MIB_2, MIB_3, MIB_4, MIB_5 = 60, 32, 24, 40, 40


def mm(a, b):
    return lax.dot_general(a, b, (((1,), (0,)), ((), ())), preferred_element_type=F32)


def mm_nt(a, b):
    return lax.dot_general(a, b, (((1,), (1,)), ((), ())), preferred_element_type=F32)


def mm_tn(a, b):
    return lax.dot_general(a, b, (((0,), (0,)), ((), ())), preferred_element_type=F32)


def one_hot(row, count):
    n = row.shape[1]
    at = lax.broadcasted_iota(I32, (count, n), 0).astype(BF16)
    hit = at == jnp.broadcast_to(row.astype(BF16), (count, n))
    return jnp.where(hit, jnp.ones((), BF16), jnp.zeros((), BF16))


def one_hot_wide(row, count):
    return jnp.concatenate(
        [one_hot(jnp.clip(row - at, -1, 256), 256) for at in range(0, count, 256)], axis=0
    )


def half_stack(m):
    return jnp.concatenate([m[:, :256], m[:, 256:]], axis=0)


def pick_fine(stack, hot, row):
    both = mm(stack, hot)
    return jnp.where(row < 256, both[:RANK], both[RANK:])


def split_rows(values):
    high = values.astype(BF16)
    low = (values - high.astype(F32)).astype(BF16)
    return jnp.concatenate([high, low], axis=0)


def spread_fine(values, row):
    first = jnp.where(row < 256, values, 0.0)
    second = jnp.where(row < 256, 0.0, values)
    return split_rows(jnp.concatenate([first, second], axis=0))


def prefix_matrix():
    down = lax.broadcasted_iota(I32, (128, 256), 0)
    across = lax.broadcasted_iota(I32, (128, 256), 1)
    return jnp.where((down <= across) | (across >= 128), 1.0, 0.0).astype(BF16)


def fetch(pairs, sems):
    copies = [pltpu.make_async_copy(a, b, sems.at[i]) for i, (a, b) in enumerate(pairs)]
    for copy in copies:
        copy.start()
    for copy in copies:
        copy.wait()


def route_kernel(
    f_owner_in, f_boxes_in, c_owner_in, c_boxes_in, slots_ref, f_pos, c_pos,
    f_owner, f_boxes, c_owner, c_boxes, sems,
):
    fetch(
        [(f_owner_in, f_owner), (f_boxes_in, f_boxes), (c_owner_in, c_owner), (c_boxes_in, c_boxes)],
        sems,
    )
    f_blocks, c_blocks = f_owner.shape[1] // 128, c_owner.shape[1] // 128
    hits = [
        lax.broadcasted_iota(I32, (DEV, 128), 0) == ref[:, b * 128:(b + 1) * 128]
        for ref, blocks in ((f_owner, f_blocks), (c_owner, c_blocks))
        for b in range(blocks)
    ]
    hots = [jnp.where(hit, 1.0, 0.0).astype(BF16) for hit in hits]
    counts = mm(jnp.concatenate(hots, axis=0), prefix_matrix())

    def place(boxes_ref, pos_ref, start, blocks, cap, wide):
        carry = jnp.zeros((DEV, 128), F32)
        parts = []
        for b in range(blocks):
            lanes = slice(b * 128, (b + 1) * 128)
            count = counts[(start + b) * 128:(start + b + 1) * 128]
            seen = count[:, :128] + carry
            pos = jnp.sum(jnp.where(hits[start + b], seen, 0.0), axis=0, keepdims=True) - 1.0
            carry = carry + count[:, 128:]
            pos = pos.astype(I32)
            pos_ref[:, lanes] = pos
            slot = boxes_ref[1:2, lanes]
            here = lax.broadcasted_iota(I32, (cap, 128), 0) == pos
            low = jnp.where(here, (slot & 255).astype(F32), 0.0)
            if wide:
                high = jnp.where(here, (slot >> 8).astype(F32), 0.0)
                low = jnp.concatenate([low, high], axis=0)
            parts.append(low.astype(BF16))
        table = mm_nt(
            jnp.concatenate(parts, axis=1), jnp.concatenate(hots[start:start + blocks], axis=1)
        )
        if wide:
            table = table[:cap] + 256.0 * table[cap:]
        return table

    fine = place(f_boxes, f_pos, 0, f_blocks, CAP_F, True)
    coarse = place(c_boxes, c_pos, f_blocks, c_blocks, CAP_C, False)
    rest = jnp.zeros((128 - CAP_F - CAP_C, DEV), F32)
    table = jnp.concatenate([fine, coarse, rest], axis=0)
    slots_ref[:, 0, :] = jnp.transpose(table).astype(I32)


def pick_operators(ops, kinds, flat, out):
    groups, nt = kinds.shape[0], ops.shape[2]
    hot = jnp.where(kinds[:, 0:1] == lax.broadcasted_iota(I32, (groups, nt), 1), 1.0, 0.0)
    hot = hot.astype(BF16)
    for quad in range(RANK // 4):
        rows = ops[quad * 4:(quad + 1) * 4].reshape(256, nt)
        got = mm_nt(hot, rows)
        for k in range(4):
            flat[pl.ds(quad * 4 + k, groups, stride=RANK), :] = got[:, k * RANK:(k + 1) * RANK]
    out[...] = flat[...].reshape(groups, RANK, RANK).astype(BF16)


def outgoing_kernel(
    ops, s_ff, s_fc, fm, cm, f_owner, f_boxes, f_pos, c_owner, c_boxes, c_pos,
    sel_ref, f_part, c_part, kinds, kf, pm, hot_out, flat,
):
    kinds[...] = jnp.zeros_like(kinds)
    kinds[0:G_FAR_F] = s_ff[...]
    kinds[G_FAR_F:G_FAR_F + G_FAR_C] = s_fc[...]
    pick_operators(ops, kinds, kf, sel_ref)

    row = c_boxes[0:1, :]
    vec = mm(cm[...], one_hot(row, 64)).astype(BF16)
    part = jnp.concatenate(
        [
            mm_tn(sel_ref[G_FAR_F + g], vec[:, g * 128:(g + 1) * 128])
            for g in range(G_FAR_C)
        ],
        axis=1,
    )
    pos = c_pos[...]
    pieces = [jnp.where(pos == k, part, 0.0).astype(BF16) for k in range(CAP_C)]
    big = mm_nt(jnp.concatenate(pieces, axis=0), one_hot(c_owner[...], DEV))
    for kp in range(ROWS_C):
        c_part[kp] = jnp.transpose(big[kp * 128:(kp + 1) * 128])

    stack = half_stack(fm[...])
    row = f_boxes[0:1, :]
    vec = pick_fine(stack, one_hot(row & 255, 256), row).astype(BF16)
    part = jnp.concatenate(
        [
            mm_tn(sel_ref[g], vec[:, g * 128:(g + 1) * 128])
            for g in range(G_FAR_F)
        ],
        axis=1,
    )
    part = (2.0 * part).astype(BF16)
    pos = f_pos[...]
    hot_out[...] = one_hot((pos >> 4) * DEV + f_owner[...], 2 * DEV)
    step = jnp.broadcast_to((pos & (HALF_CAP - 1)).astype(BF16), part.shape)
    none = jnp.zeros((), BF16)
    for k in range(HALF_CAP):
        pm[k * RANK:(k + 1) * RANK, :] = jnp.where(step == jnp.asarray(k, BF16), part, none)
    for j in range(HALF_CAP * RANK // PM_ROWS):
        big = mm_nt(pm[j * PM_ROWS:(j + 1) * PM_ROWS, :], hot_out[...])
        for i in range(PM_ROWS // 128):
            kp = j * (PM_ROWS // 128) + i
            for half in range(2):
                turned = jnp.transpose(big[i * 128:(i + 1) * 128, half * DEV:(half + 1) * DEV])
                flat[pl.ds(half * (HALF_CAP // 2) + kp, DEV, stride=ROWS_F), :] = turned

    f_part[...] = flat[...].reshape(DEV, ROWS_F, 128).astype(BF16)


def slot_rows(slots):
    table = jnp.transpose(slots[:, 0, :].astype(F32)).astype(I32)
    rows = [table[k:k + 1] for k in range(CAP_F + CAP_C)]
    return jnp.concatenate(rows[:CAP_F], axis=1), jnp.concatenate(rows[CAP_F:], axis=1)


def reply_kernel(slots, fm, cm, f_part, c_part, out_ref, f_flat, c_flat):
    f_row, c_row = slot_rows(slots)
    f_vec = pick_fine(half_stack(fm[...]), one_hot(f_row & 255, 256), f_row)
    c_vec = mm(cm[...], one_hot(c_row, 64))

    def turned(vec, kp):
        at = 2 * kp * DEV
        return jnp.transpose(
            jnp.concatenate([vec[:, at:at + DEV], vec[:, at + DEV:at + 2 * DEV]], axis=0)
        )

    for kp in range(ROWS_F):
        f_flat[pl.ds(kp, DEV, stride=ROWS_F), :] = turned(f_vec, kp)
    for kp in range(ROWS_C):
        c_flat[pl.ds(kp, DEV, stride=2 * ROWS_C), :] = turned(c_vec, kp)
        c_flat[pl.ds(ROWS_C + kp, DEV, stride=2 * ROWS_C), :] = c_part[kp]
    out_ref[...] = jnp.concatenate(
        [
            f_flat[...].reshape(DEV, ROWS_F, 128).astype(BF16),
            f_part[...],
            c_flat[...].reshape(DEV, 2 * ROWS_C, 128).astype(BF16),
        ],
        axis=1,
    )


def near_kernel(ops, s_nf, s_nc, fm, cm, f_boxes, c_boxes, f_out, c_out, kinds, kf, sel, f_sum):
    kinds[0:G_NEAR_F] = s_nf[...]
    kinds[G_NEAR_F:NEAR_GROUPS] = s_nc[...]
    pick_operators(ops, kinds, kf, sel)
    stack = half_stack(fm[...])
    f_sum[...] = jnp.zeros_like(f_sum)

    def step(i, carry):
        lanes = pl.ds(pl.multiple_of(i * NEAR_BLOCK, NEAR_BLOCK), NEAR_BLOCK)
        first = f_boxes[0:1, lanes]
        second = f_boxes[1:2, lanes]
        hot_1 = one_hot(first & 255, 256)
        hot_2 = one_hot(second & 255, 256)
        vec_1 = pick_fine(stack, hot_1, first).astype(BF16)
        vec_2 = pick_fine(stack, hot_2, second).astype(BF16)
        to_1, to_2 = [], []
        for k in range(NEAR_BLOCK // 128):
            op = sel[NEAR_BLOCK // 128 * i + k]
            cut = slice(k * 128, (k + 1) * 128)
            to_1.append(mm(op, vec_2[:, cut]))
            to_2.append(mm_tn(op, vec_1[:, cut]))
        to_1 = jnp.concatenate(to_1, axis=1)
        to_2 = jnp.concatenate(to_2, axis=1)
        both = jnp.concatenate([spread_fine(to_1, first), spread_fine(to_2, second)], axis=1)
        hots = jnp.concatenate([hot_1, hot_2], axis=1)
        f_sum[...] += mm_nt(both, hots)
        return carry

    lax.fori_loop(0, G_NEAR_F * 128 // NEAR_BLOCK, step, 0)
    f_out[...] = f_sum[:2 * RANK] + f_sum[2 * RANK:]
    total = jnp.zeros((2 * RANK, 64), F32)
    for g in range(G_NEAR_C):
        lanes = slice(g * 128, (g + 1) * 128)
        hot_1 = one_hot(c_boxes[0:1, lanes], 64)
        hot_2 = one_hot(c_boxes[1:2, lanes], 64)
        vec_1 = mm(cm[...], hot_1).astype(BF16)
        vec_2 = mm(cm[...], hot_2).astype(BF16)
        op = sel[G_NEAR_F + g]
        total = total + mm_nt(split_rows(mm(op, vec_2)), hot_1)
        total = total + mm_nt(split_rows(mm_tn(op, vec_1)), hot_2)
    c_out[...] = total[:RANK] + total[RANK:]


def final_kernel(
    got, slots, sel, f_near, c_near, parent, maps, f_owner, f_boxes, f_pos, c_owner, c_boxes, c_pos,
    c_ref, f_ref, flat,
):
    flat[...] = got[...].astype(F32).reshape(DEV * ROWS, 128)
    f_row, c_row = slot_rows(slots)

    def turned(row):
        return jnp.transpose(flat[pl.ds(row, DEV, stride=ROWS), :])

    def choose(found, where, count):
        vec = found[:RANK]
        for k in range(1, count):
            vec = jnp.where(where == k, found[k * RANK:(k + 1) * RANK], vec)
        return vec.astype(BF16)

    held_c = jnp.concatenate([turned(2 * ROWS_F + kp) for kp in range(ROWS_C)], axis=0)
    vec_c = choose(mm(held_c.astype(BF16), one_hot(c_owner[...], DEV)), c_pos[...], CAP_C)
    to_1 = jnp.concatenate(
        [mm(sel[G_FAR_F + g], vec_c[:, g * 128:(g + 1) * 128]) for g in range(G_FAR_C)], axis=1
    )
    far_c = mm_nt(split_rows(to_1), one_hot(c_boxes[0:1, :], 64))
    sides_c = []
    for kp in range(ROWS_C):
        arrived = turned(2 * ROWS_F + ROWS_C + kp)
        sides_c += [arrived[:RANK], arrived[RANK:]]
    arrived_c = mm_nt(jnp.concatenate(sides_c, axis=1).astype(BF16), one_hot(c_row, 64))
    coarse = parent[...] + c_near[...] + far_c[:RANK] + far_c[RANK:] + arrived_c
    coarse = coarse.astype(BF16)
    c_ref[...] = coarse

    held = jnp.concatenate(
        [
            jnp.concatenate([turned(quarter * (ROWS_F // 4) + kp) for quarter in range(4)], axis=1)
            for kp in range(ROWS_F // 4)
        ],
        axis=0,
    ).astype(BF16)
    pos = f_pos[...]
    hot = one_hot_wide((pos // PART_CAP) * DEV + f_owner[...], 4 * DEV)
    vec = choose(mm(held, hot), pos & (PART_CAP - 1), PART_CAP)
    to_1 = jnp.concatenate(
        [mm(sel[g], vec[:, g * 128:(g + 1) * 128]) for g in range(G_FAR_F)], axis=1
    )
    first = f_boxes[0:1, :]
    total = mm_nt(spread_fine(to_1, first), one_hot(first & 255, 256))
    sides = []
    for kp in range(ROWS_F):
        arrived = turned(ROWS_F + kp)
        sides += [arrived[:RANK], arrived[RANK:]]
    side = jnp.concatenate(sides, axis=1)
    side = jnp.concatenate(
        [jnp.where(f_row < 256, side, 0.0), jnp.where(f_row < 256, 0.0, side)], axis=0
    )
    added = mm_nt(side.astype(BF16), one_hot(f_row & 255, 256))

    box = lax.broadcasted_iota(I32, (64, 512), 1)
    parent_of = jnp.where((box >> 3) == lax.broadcasted_iota(I32, (64, 512), 0), 1.0, 0.0)
    wide = mm(coarse, parent_of.astype(BF16)).astype(BF16)
    starts = mm(maps[...].reshape(8 * RANK, RANK), wide)
    start = starts[:RANK]
    for k in range(1, 8):
        start = jnp.where((box & 7) == k, starts[k * RANK:(k + 1) * RANK], start)

    total = 2.0 * (f_near[...] + total[:2 * RANK] + total[2 * RANK:]) + added
    fine = start + jnp.concatenate([total[:RANK], total[RANK:]], axis=1)
    f_ref[...] = fine.astype(BF16)


def call(kernel, out_shape, scratch, mib, flops, nbytes, *args, **more):
    return pl.pallas_call(
        kernel,
        out_shape=out_shape,
        scratch_shapes=scratch,
        compiler_params=pltpu.CompilerParams(vmem_limit_bytes=mib * 1024 * 1024),
        cost_estimate=pl.CostEstimate(flops=flops, bytes_accessed=nbytes, transcendentals=0),
        **more,
    )(*args)


def on_device(
    coarse_multipole,
    fine_multipole,
    parent_local,
    operators,
    child_maps,
    coarse_near_boxes,
    coarse_near_shift,
    coarse_far_boxes,
    coarse_far_owner,
    coarse_far_shift,
    fine_near_boxes,
    fine_near_shift,
    fine_far_boxes,
    fine_far_owner,
    fine_far_shift,
):
    def sds(shape, dtype):
        return jax.ShapeDtypeStruct(shape, dtype)

    fm, cm = fine_multipole, coarse_multipole
    f_owner, c_owner = fine_far_owner.T, coarse_far_owner.T
    f_far, c_far = fine_far_boxes.T, coarse_far_boxes.T
    ops = jnp.transpose(operators, (1, 2, 0))

    n_f, n_c = f_owner.shape[1], c_owner.shape[1]
    slots, f_pos, c_pos = call(
        route_kernel,
        (sds((DEV, 1, 128), I32), sds((1, n_f), I32), sds((1, n_c), I32)),
        [
            pltpu.VMEM((1, n_f), I32),
            pltpu.VMEM((2, n_f), I32),
            pltpu.VMEM((1, n_c), I32),
            pltpu.VMEM((2, n_c), I32),
            pltpu.SemaphoreType.DMA((4,)),
        ],
        MIB_1,
        10**9,
        10**6,
        f_owner, f_far, c_owner, c_far,
        in_specs=[pl.BlockSpec(memory_space=pltpu.HBM)] * 4,
    )
    asked = lax.all_to_all(slots, ("oct", "box"), split_axis=0, concat_axis=0, tiled=True)
    sel, f_part, c_part = call(
        outgoing_kernel,
        (
            sds((FAR_GROUPS, RANK, RANK), BF16),
            sds((DEV, ROWS_F, 128), BF16),
            sds((ROWS_C, DEV, 128), F32),
        ),
        [
            pltpu.VMEM((FAR_GROUPS, 128), I32),
            pltpu.VMEM((FAR_GROUPS * RANK, RANK), F32),
            pltpu.VMEM((HALF_CAP * RANK, n_f), BF16),
            pltpu.VMEM((2 * DEV, n_f), BF16),
            pltpu.VMEM((DEV * ROWS_F, 128), F32),
        ],
        MIB_2,
        5 * 10**9,
        10**7,
        ops,
        fine_far_shift.reshape(-1, 128),
        coarse_far_shift.reshape(-1, 128),
        fm, cm, f_owner, f_far, f_pos, c_owner, c_far, c_pos,
    )
    sent = call(
        reply_kernel,
        sds((DEV, ROWS, 128), BF16),
        [pltpu.VMEM((DEV * ROWS_F, 128), F32), pltpu.VMEM((DEV * 2 * ROWS_C, 128), F32)],
        MIB_3,
        10**9,
        10**6,
        asked, fm, cm, f_part, c_part,
    )
    got = lax.all_to_all(sent, ("oct", "box"), split_axis=0, concat_axis=0, tiled=True)
    f_near, c_near = call(
        near_kernel,
        (sds((2 * RANK, 256), F32), sds((RANK, 64), F32)),
        [
            pltpu.VMEM((NEAR_GROUPS, 128), I32),
            pltpu.VMEM((NEAR_GROUPS * RANK, RANK), F32),
            pltpu.VMEM((NEAR_GROUPS, RANK, RANK), BF16),
            pltpu.VMEM((4 * RANK, 256), F32),
        ],
        MIB_4,
        10**10,
        10**7,
        ops,
        fine_near_shift.reshape(-1, 128),
        coarse_near_shift.reshape(-1, 128),
        fm, cm, fine_near_boxes.T, coarse_near_boxes.T,
    )
    return call(
        final_kernel,
        (sds((RANK, 64), BF16), sds((RANK, 512), BF16)),
        [pltpu.VMEM((DEV * ROWS, 128), F32)],
        MIB_5,
        3 * 10**9,
        10**7,
        got, asked, sel, f_near, c_near, parent_local, child_maps,
        f_owner, f_far, f_pos, c_owner, c_far, c_pos,
    )


def solution(mesh):
    both = ("oct", "box")
    return jax.shard_map(
        on_device,
        mesh=mesh,
        in_specs=(
            P(None, both),
            P(None, both),
            P(None, both),
            P(),
            P(),
            P(both, None),
            P(both),
            P(both, None),
            P(both, None),
            P(both),
            P(both, None),
            P(both),
            P(both, None),
            P(both, None),
            P(both),
        ),
        out_specs=(P(None, both), P(None, both)),
        check_vma=False,
    )
```

```python
import jax
import jax.numpy as jnp
from jax import lax
from jax.experimental import pallas as pl
from jax.experimental.pallas import tpu as pltpu
from jax.sharding import PartitionSpec as P


F32 = jnp.float32
BF16 = jnp.bfloat16
I32 = jnp.int32

DEV = 128
RANK = 64
CAP_F = 32
CAP_C = 8
ROWS_F = CAP_F * RANK // 128
ROWS_C = CAP_C * RANK // 128
ROWS = 2 * (ROWS_F + ROWS_C)
HALF_CAP = CAP_F // 2
PART_CAP = CAP_F // 4
G_NEAR_F, G_FAR_F, G_NEAR_C, G_FAR_C = 64, 16, 8, 4
FAR_GROUPS = 24
NEAR_GROUPS = G_NEAR_F + G_NEAR_C
NEAR_BLOCK = 4096
PM_ROWS = 512
MIB_1, MIB_2, MIB_3, MIB_4, MIB_5 = 16, 32, 24, 40, 40


def mm(a, b):
    return lax.dot_general(a, b, (((1,), (0,)), ((), ())), preferred_element_type=F32)


def mm_nt(a, b):
    return lax.dot_general(a, b, (((1,), (1,)), ((), ())), preferred_element_type=F32)


def mm_tn(a, b):
    return lax.dot_general(a, b, (((0,), (0,)), ((), ())), preferred_element_type=F32)


def one_hot(row, count):
    n = row.shape[1]
    at = lax.broadcasted_iota(I32, (count, n), 0).astype(BF16)
    hit = at == jnp.broadcast_to(row.astype(BF16), (count, n))
    return jnp.where(hit, jnp.ones((), BF16), jnp.zeros((), BF16))


def one_hot_wide(row, count):
    return jnp.concatenate(
        [one_hot(jnp.clip(row - at, -1, 256), 256) for at in range(0, count, 256)], axis=0
    )


def half_stack(m):
    return jnp.concatenate([m[:, :256], m[:, 256:]], axis=0)


def pick_fine(stack, hot, row):
    both = mm(stack, hot)
    return jnp.where(row < 256, both[:RANK], both[RANK:])


def split_rows(values):
    high = values.astype(BF16)
    low = (values - high.astype(F32)).astype(BF16)
    return jnp.concatenate([high, low], axis=0)


def spread_fine(values, row):
    first = jnp.where(row < 256, values, 0.0)
    second = jnp.where(row < 256, 0.0, values)
    return split_rows(jnp.concatenate([first, second], axis=0))


def prefix_matrix():
    down = lax.broadcasted_iota(I32, (128, 256), 0)
    across = lax.broadcasted_iota(I32, (128, 256), 1)
    return jnp.where((down <= across) | (across >= 128), 1.0, 0.0).astype(BF16)


def route_kernel(
    f_owner_in, f_boxes_in, c_owner_in, c_boxes_in, ops_in,
    slots_ref, f_pos, c_pos, f_owner, f_boxes, c_owner, c_boxes, ops,
    sems,
):
    copies = [
        pltpu.make_async_copy(source, target, sems.at[i])
        for i, (source, target) in enumerate(
            [
                (f_owner_in, f_owner),
                (c_owner_in, c_owner),
                (f_boxes_in, f_boxes),
                (c_boxes_in, c_boxes),
                (ops_in, ops),
            ]
        )
    ]
    for copy in copies:
        copy.start()
    for copy in copies[:4]:
        copy.wait()
    f_blocks, c_blocks = f_owner.shape[1] // 128, c_owner.shape[1] // 128
    hits = [
        lax.broadcasted_iota(I32, (DEV, 128), 0) == ref[:, b * 128:(b + 1) * 128]
        for ref, blocks in ((f_owner, f_blocks), (c_owner, c_blocks))
        for b in range(blocks)
    ]
    hots = [jnp.where(hit, 1.0, 0.0).astype(BF16) for hit in hits]
    counts = mm(jnp.concatenate(hots, axis=0), prefix_matrix())

    def place(boxes_ref, pos_ref, start, blocks, cap, wide):
        carry = jnp.zeros((DEV, 128), F32)
        parts = []
        for b in range(blocks):
            lanes = slice(b * 128, (b + 1) * 128)
            count = counts[(start + b) * 128:(start + b + 1) * 128]
            seen = count[:, :128] + carry
            pos = jnp.sum(jnp.where(hits[start + b], seen, 0.0), axis=0, keepdims=True) - 1.0
            carry = carry + count[:, 128:]
            pos = pos.astype(I32)
            pos_ref[:, lanes] = pos
            slot = boxes_ref[1:2, lanes]
            here = lax.broadcasted_iota(I32, (cap, 128), 0) == pos
            low = jnp.where(here, (slot & 255).astype(F32), 0.0)
            if wide:
                high = jnp.where(here, (slot >> 8).astype(F32), 0.0)
                low = jnp.concatenate([low, high], axis=0)
            parts.append(low.astype(BF16))
        table = mm_nt(
            jnp.concatenate(parts, axis=1), jnp.concatenate(hots[start:start + blocks], axis=1)
        )
        if wide:
            table = table[:cap] + 256.0 * table[cap:]
        return table

    fine = place(f_boxes, f_pos, 0, f_blocks, CAP_F, True)
    coarse = place(c_boxes, c_pos, f_blocks, c_blocks, CAP_C, False)
    rest = jnp.zeros((128 - CAP_F - CAP_C, DEV), F32)
    table = jnp.concatenate([fine, coarse, rest], axis=0)
    slots_ref[:, 0, :] = jnp.transpose(table).astype(I32)
    copies[4].wait()


def pick_operators(ops, kinds, flat, out):
    groups, nt = kinds.shape[0], ops.shape[2]
    hot = jnp.where(kinds[:, 0:1] == lax.broadcasted_iota(I32, (groups, nt), 1), 1.0, 0.0)
    hot = hot.astype(BF16)
    for quad in range(RANK // 4):
        rows = ops[quad * 4:(quad + 1) * 4].reshape(256, nt)
        got = mm_nt(hot, rows)
        for k in range(4):
            flat[pl.ds(quad * 4 + k, groups, stride=RANK), :] = got[:, k * RANK:(k + 1) * RANK]
    out[...] = flat[...].reshape(groups, RANK, RANK).astype(BF16)


def outgoing_kernel(
    ops, s_ff, s_fc, fm, cm, f_owner, f_boxes, f_pos, c_owner, c_boxes, c_pos,
    sel_ref, f_part, c_part, kinds, kf, pm, hot_out, flat,
):
    kinds[...] = jnp.zeros_like(kinds)
    kinds[0:G_FAR_F] = s_ff[...]
    kinds[G_FAR_F:G_FAR_F + G_FAR_C] = s_fc[...]
    pick_operators(ops, kinds, kf, sel_ref)

    row = c_boxes[0:1, :]
    vec = mm(cm[...], one_hot(row, 64)).astype(BF16)
    part = jnp.concatenate(
        [
            mm_tn(sel_ref[G_FAR_F + g], vec[:, g * 128:(g + 1) * 128])
            for g in range(G_FAR_C)
        ],
        axis=1,
    )
    pos = c_pos[...]
    pieces = [jnp.where(pos == k, part, 0.0).astype(BF16) for k in range(CAP_C)]
    big = mm_nt(jnp.concatenate(pieces, axis=0), one_hot(c_owner[...], DEV))
    for kp in range(ROWS_C):
        c_part[kp] = jnp.transpose(big[kp * 128:(kp + 1) * 128])

    stack = half_stack(fm[...])
    row = f_boxes[0:1, :]
    vec = pick_fine(stack, one_hot(row & 255, 256), row).astype(BF16)
    part = jnp.concatenate(
        [
            mm_tn(sel_ref[g], vec[:, g * 128:(g + 1) * 128])
            for g in range(G_FAR_F)
        ],
        axis=1,
    )
    part = (2.0 * part).astype(BF16)
    pos = f_pos[...]
    hot_out[...] = one_hot((pos >> 4) * DEV + f_owner[...], 2 * DEV)
    step = jnp.broadcast_to((pos & (HALF_CAP - 1)).astype(BF16), part.shape)
    none = jnp.zeros((), BF16)
    for k in range(HALF_CAP):
        pm[k * RANK:(k + 1) * RANK, :] = jnp.where(step == jnp.asarray(k, BF16), part, none)
    for j in range(HALF_CAP * RANK // PM_ROWS):
        big = mm_nt(pm[j * PM_ROWS:(j + 1) * PM_ROWS, :], hot_out[...])
        for i in range(PM_ROWS // 128):
            kp = j * (PM_ROWS // 128) + i
            for half in range(2):
                turned = jnp.transpose(big[i * 128:(i + 1) * 128, half * DEV:(half + 1) * DEV])
                flat[pl.ds(half * (HALF_CAP // 2) + kp, DEV, stride=ROWS_F), :] = turned

    f_part[...] = flat[...].reshape(DEV, ROWS_F, 128).astype(BF16)


def slot_rows(slots):
    table = jnp.transpose(slots[:, 0, :].astype(F32)).astype(I32)
    rows = [table[k:k + 1] for k in range(CAP_F + CAP_C)]
    return jnp.concatenate(rows[:CAP_F], axis=1), jnp.concatenate(rows[CAP_F:], axis=1)


def reply_kernel(slots, fm, cm, f_part, c_part, out_ref, f_flat, c_flat):
    f_row, c_row = slot_rows(slots)
    f_vec = pick_fine(half_stack(fm[...]), one_hot(f_row & 255, 256), f_row)
    c_vec = mm(cm[...], one_hot(c_row, 64))

    def turned(vec, kp):
        at = 2 * kp * DEV
        return jnp.transpose(
            jnp.concatenate([vec[:, at:at + DEV], vec[:, at + DEV:at + 2 * DEV]], axis=0)
        )

    for kp in range(ROWS_F):
        f_flat[pl.ds(kp, DEV, stride=ROWS_F), :] = turned(f_vec, kp)
    for kp in range(ROWS_C):
        c_flat[pl.ds(kp, DEV, stride=2 * ROWS_C), :] = turned(c_vec, kp)
        c_flat[pl.ds(ROWS_C + kp, DEV, stride=2 * ROWS_C), :] = c_part[kp]
    out_ref[...] = jnp.concatenate(
        [
            f_flat[...].reshape(DEV, ROWS_F, 128).astype(BF16),
            f_part[...],
            c_flat[...].reshape(DEV, 2 * ROWS_C, 128).astype(BF16),
        ],
        axis=1,
    )


def near_kernel(ops, s_nf, s_nc, fm, cm, f_boxes, c_boxes, f_out, c_out, kinds, kf, sel, f_sum):
    kinds[0:G_NEAR_F] = s_nf[...]
    kinds[G_NEAR_F:NEAR_GROUPS] = s_nc[...]
    pick_operators(ops, kinds, kf, sel)
    stack = half_stack(fm[...])
    f_sum[...] = jnp.zeros_like(f_sum)

    def step(i, carry):
        lanes = pl.ds(pl.multiple_of(i * NEAR_BLOCK, NEAR_BLOCK), NEAR_BLOCK)
        first = f_boxes[0:1, lanes]
        second = f_boxes[1:2, lanes]
        hot_1 = one_hot(first & 255, 256)
        hot_2 = one_hot(second & 255, 256)
        vec_1 = pick_fine(stack, hot_1, first).astype(BF16)
        vec_2 = pick_fine(stack, hot_2, second).astype(BF16)
        to_1, to_2 = [], []
        for k in range(NEAR_BLOCK // 128):
            op = sel[NEAR_BLOCK // 128 * i + k]
            cut = slice(k * 128, (k + 1) * 128)
            to_1.append(mm(op, vec_2[:, cut]))
            to_2.append(mm_tn(op, vec_1[:, cut]))
        to_1 = jnp.concatenate(to_1, axis=1)
        to_2 = jnp.concatenate(to_2, axis=1)
        both = jnp.concatenate([spread_fine(to_1, first), spread_fine(to_2, second)], axis=1)
        hots = jnp.concatenate([hot_1, hot_2], axis=1)
        f_sum[...] += mm_nt(both, hots)
        return carry

    lax.fori_loop(0, G_NEAR_F * 128 // NEAR_BLOCK, step, 0)
    f_out[...] = f_sum[:2 * RANK] + f_sum[2 * RANK:]
    total = jnp.zeros((2 * RANK, 64), F32)
    for g in range(G_NEAR_C):
        lanes = slice(g * 128, (g + 1) * 128)
        hot_1 = one_hot(c_boxes[0:1, lanes], 64)
        hot_2 = one_hot(c_boxes[1:2, lanes], 64)
        vec_1 = mm(cm[...], hot_1).astype(BF16)
        vec_2 = mm(cm[...], hot_2).astype(BF16)
        op = sel[G_NEAR_F + g]
        total = total + mm_nt(split_rows(mm(op, vec_2)), hot_1)
        total = total + mm_nt(split_rows(mm_tn(op, vec_1)), hot_2)
    c_out[...] = total[:RANK] + total[RANK:]


def final_kernel(
    got, slots, sel, f_near, c_near, parent, maps, f_owner, f_boxes, f_pos, c_owner, c_boxes, c_pos,
    c_ref, f_ref, flat,
):
    flat[...] = got[...].astype(F32).reshape(DEV * ROWS, 128)
    f_row, c_row = slot_rows(slots)

    def turned(row):
        return jnp.transpose(flat[pl.ds(row, DEV, stride=ROWS), :])

    def choose(found, where, count):
        vec = found[:RANK]
        for k in range(1, count):
            vec = jnp.where(where == k, found[k * RANK:(k + 1) * RANK], vec)
        return vec.astype(BF16)

    held_c = jnp.concatenate([turned(2 * ROWS_F + kp) for kp in range(ROWS_C)], axis=0)
    vec_c = choose(mm(held_c.astype(BF16), one_hot(c_owner[...], DEV)), c_pos[...], CAP_C)
    to_1 = jnp.concatenate(
        [mm(sel[G_FAR_F + g], vec_c[:, g * 128:(g + 1) * 128]) for g in range(G_FAR_C)], axis=1
    )
    far_c = mm_nt(split_rows(to_1), one_hot(c_boxes[0:1, :], 64))
    sides_c = []
    for kp in range(ROWS_C):
        arrived = turned(2 * ROWS_F + ROWS_C + kp)
        sides_c += [arrived[:RANK], arrived[RANK:]]
    arrived_c = mm_nt(jnp.concatenate(sides_c, axis=1).astype(BF16), one_hot(c_row, 64))
    coarse = parent[...] + c_near[...] + far_c[:RANK] + far_c[RANK:] + arrived_c
    coarse = coarse.astype(BF16)
    c_ref[...] = coarse

    held = jnp.concatenate(
        [
            jnp.concatenate([turned(quarter * (ROWS_F // 4) + kp) for quarter in range(4)], axis=1)
            for kp in range(ROWS_F // 4)
        ],
        axis=0,
    ).astype(BF16)
    pos = f_pos[...]
    hot = one_hot_wide((pos // PART_CAP) * DEV + f_owner[...], 4 * DEV)
    vec = choose(mm(held, hot), pos & (PART_CAP - 1), PART_CAP)
    to_1 = jnp.concatenate(
        [mm(sel[g], vec[:, g * 128:(g + 1) * 128]) for g in range(G_FAR_F)], axis=1
    )
    first = f_boxes[0:1, :]
    total = mm_nt(spread_fine(to_1, first), one_hot(first & 255, 256))
    sides = []
    for kp in range(ROWS_F):
        arrived = turned(ROWS_F + kp)
        sides += [arrived[:RANK], arrived[RANK:]]
    side = jnp.concatenate(sides, axis=1)
    side = jnp.concatenate(
        [jnp.where(f_row < 256, side, 0.0), jnp.where(f_row < 256, 0.0, side)], axis=0
    )
    added = mm_nt(side.astype(BF16), one_hot(f_row & 255, 256))

    box = lax.broadcasted_iota(I32, (64, 512), 1)
    parent_of = jnp.where((box >> 3) == lax.broadcasted_iota(I32, (64, 512), 0), 1.0, 0.0)
    wide = mm(coarse, parent_of.astype(BF16)).astype(BF16)
    starts = mm(maps[...].reshape(8 * RANK, RANK), wide)
    start = starts[:RANK]
    for k in range(1, 8):
        start = jnp.where((box & 7) == k, starts[k * RANK:(k + 1) * RANK], start)

    total = 2.0 * (f_near[...] + total[:2 * RANK] + total[2 * RANK:]) + added
    fine = start + jnp.concatenate([total[:RANK], total[RANK:]], axis=1)
    f_ref[...] = fine.astype(BF16)


def call(kernel, out_shape, scratch, mib, flops, nbytes, *args, **more):
    return pl.pallas_call(
        kernel,
        out_shape=out_shape,
        scratch_shapes=scratch,
        compiler_params=pltpu.CompilerParams(vmem_limit_bytes=mib * 1024 * 1024),
        cost_estimate=pl.CostEstimate(flops=flops, bytes_accessed=nbytes, transcendentals=0),
        **more,
    )(*args)


def on_device(
    coarse_multipole,
    fine_multipole,
    parent_local,
    operators,
    child_maps,
    coarse_near_boxes,
    coarse_near_shift,
    coarse_far_boxes,
    coarse_far_owner,
    coarse_far_shift,
    fine_near_boxes,
    fine_near_shift,
    fine_far_boxes,
    fine_far_owner,
    fine_far_shift,
):
    def sds(shape, dtype):
        return jax.ShapeDtypeStruct(shape, dtype)

    fm, cm = fine_multipole, coarse_multipole
    f_owner, c_owner = fine_far_owner.T, coarse_far_owner.T
    f_far, c_far = fine_far_boxes.T, coarse_far_boxes.T
    ops = jnp.transpose(operators, (1, 2, 0))

    n_f, n_c = f_owner.shape[1], c_owner.shape[1]
    slots, f_pos, c_pos, f_owner, f_far, c_owner, c_far, ops = call(
        route_kernel,
        (
            sds((DEV, 1, 128), I32),
            pltpu.VMEM((1, n_f), I32),
            pltpu.VMEM((1, n_c), I32),
            pltpu.VMEM((1, n_f), I32),
            pltpu.VMEM((2, n_f), I32),
            pltpu.VMEM((1, n_c), I32),
            pltpu.VMEM((2, n_c), I32),
            pltpu.VMEM(ops.shape, BF16),
        ),
        [pltpu.SemaphoreType.DMA((5,))],
        MIB_1,
        10**9,
        10**6,
        *[
            pltpu.with_memory_space_constraint(x, pltpu.HBM)
            for x in (f_owner, f_far, c_owner, c_far, ops)
        ],
        in_specs=[pl.BlockSpec(memory_space=pltpu.HBM)] * 5,
    )
    asked = lax.all_to_all(slots, ("oct", "box"), split_axis=0, concat_axis=0, tiled=True)
    sel, f_part, c_part = call(
        outgoing_kernel,
        (
            sds((FAR_GROUPS, RANK, RANK), BF16),
            sds((DEV, ROWS_F, 128), BF16),
            sds((ROWS_C, DEV, 128), F32),
        ),
        [
            pltpu.VMEM((FAR_GROUPS, 128), I32),
            pltpu.VMEM((FAR_GROUPS * RANK, RANK), F32),
            pltpu.VMEM((HALF_CAP * RANK, n_f), BF16),
            pltpu.VMEM((2 * DEV, n_f), BF16),
            pltpu.VMEM((DEV * ROWS_F, 128), F32),
        ],
        MIB_2,
        5 * 10**9,
        10**7,
        ops,
        fine_far_shift.reshape(-1, 128),
        coarse_far_shift.reshape(-1, 128),
        fm, cm, f_owner, f_far, f_pos, c_owner, c_far, c_pos,
    )
    sent = call(
        reply_kernel,
        pltpu.VMEM((DEV, ROWS, 128), BF16),
        [pltpu.VMEM((DEV * ROWS_F, 128), F32), pltpu.VMEM((DEV * 2 * ROWS_C, 128), F32)],
        MIB_3,
        10**9,
        10**6,
        asked, fm, cm, f_part, c_part,
    )
    got = lax.all_to_all(sent, ("oct", "box"), split_axis=0, concat_axis=0, tiled=True)
    f_near, c_near = call(
        near_kernel,
        (sds((2 * RANK, 256), F32), sds((RANK, 64), F32)),
        [
            pltpu.VMEM((NEAR_GROUPS, 128), I32),
            pltpu.VMEM((NEAR_GROUPS * RANK, RANK), F32),
            pltpu.VMEM((NEAR_GROUPS, RANK, RANK), BF16),
            pltpu.VMEM((4 * RANK, 256), F32),
        ],
        MIB_4,
        10**10,
        10**7,
        ops,
        fine_near_shift.reshape(-1, 128),
        coarse_near_shift.reshape(-1, 128),
        fm, cm, fine_near_boxes.T, coarse_near_boxes.T,
    )
    return call(
        final_kernel,
        (sds((RANK, 64), BF16), sds((RANK, 512), BF16)),
        [pltpu.VMEM((DEV * ROWS, 128), F32)],
        MIB_5,
        3 * 10**9,
        10**7,
        got, asked, sel, f_near, c_near, parent_local, child_maps,
        f_owner, f_far, f_pos, c_owner, c_far, c_pos,
    )


def solution(mesh):
    both = ("oct", "box")
    return jax.shard_map(
        on_device,
        mesh=mesh,
        in_specs=(
            P(None, both),
            P(None, both),
            P(None, both),
            P(),
            P(),
            P(both, None),
            P(both),
            P(both, None),
            P(both, None),
            P(both),
            P(both, None),
            P(both),
            P(both, None),
            P(both, None),
            P(both),
        ),
        out_specs=(P(None, both), P(None, both)),
        check_vma=False,
    )
```

```python
import jax
import jax.numpy as jnp
from jax import lax
from jax.experimental import pallas as pl
from jax.experimental.pallas import tpu as pltpu
from jax.sharding import PartitionSpec as P


F32 = jnp.float32
BF16 = jnp.bfloat16
I32 = jnp.int32

DEV = 128
RANK = 64
CAP_F = 32
CAP_C = 8
ROWS_F = CAP_F * RANK // 128
ROWS_C = CAP_C * RANK // 128
ROWS = 2 * (ROWS_F + ROWS_C)
HALF_CAP = CAP_F // 2
PART_CAP = CAP_F // 4
G_NEAR_F, G_FAR_F, G_NEAR_C, G_FAR_C = 64, 16, 8, 4
FAR_GROUPS = 24
NEAR_GROUPS = G_NEAR_F + G_NEAR_C
NEAR_BLOCK = 4096
PM_ROWS = 512
OPS_CHUNKS = 2
MIB_1, MIB_2, MIB_3, MIB_4, MIB_5 = 16, 36, 24, 44, 40


def mm(a, b):
    return lax.dot_general(a, b, (((1,), (0,)), ((), ())), preferred_element_type=F32)


def mm_nt(a, b):
    return lax.dot_general(a, b, (((1,), (1,)), ((), ())), preferred_element_type=F32)


def mm_tn(a, b):
    return lax.dot_general(a, b, (((0,), (0,)), ((), ())), preferred_element_type=F32)


def one_hot(row, count):
    n = row.shape[1]
    at = lax.broadcasted_iota(I32, (count, n), 0).astype(BF16)
    hit = at == jnp.broadcast_to(row.astype(BF16), (count, n))
    return jnp.where(hit, jnp.ones((), BF16), jnp.zeros((), BF16))


def one_hot_wide(row, count):
    return jnp.concatenate(
        [one_hot(jnp.clip(row - at, -1, 256), 256) for at in range(0, count, 256)], axis=0
    )


def half_stack(m):
    return jnp.concatenate([m[:, :256], m[:, 256:]], axis=0)


def pick_fine(stack, hot, row):
    both = mm(stack, hot)
    return jnp.where(row < 256, both[:RANK], both[RANK:])


def split_rows(values):
    high = values.astype(BF16)
    low = (values - high.astype(F32)).astype(BF16)
    return jnp.concatenate([high, low], axis=0)


def spread_fine(values, row):
    first = jnp.where(row < 256, values, 0.0)
    second = jnp.where(row < 256, 0.0, values)
    return split_rows(jnp.concatenate([first, second], axis=0))


def prefix_matrix():
    down = lax.broadcasted_iota(I32, (128, 256), 0)
    across = lax.broadcasted_iota(I32, (128, 256), 1)
    return jnp.where((down <= across) | (across >= 128), 1.0, 0.0).astype(BF16)


def route_kernel(
    f_owner_in, f_boxes_in, c_owner_in, c_boxes_in,
    slots_ref, f_pos, c_pos, f_owner, f_boxes, c_owner, c_boxes, sems,
):
    copies = [
        pltpu.make_async_copy(source, target, sems.at[i])
        for i, (source, target) in enumerate(
            [
                (f_owner_in, f_owner),
                (c_owner_in, c_owner),
                (f_boxes_in, f_boxes),
                (c_boxes_in, c_boxes),
            ]
        )
    ]
    for copy in copies:
        copy.start()
    for copy in copies:
        copy.wait()
    f_blocks, c_blocks = f_owner.shape[1] // 128, c_owner.shape[1] // 128
    hits = [
        lax.broadcasted_iota(I32, (DEV, 128), 0) == ref[:, b * 128:(b + 1) * 128]
        for ref, blocks in ((f_owner, f_blocks), (c_owner, c_blocks))
        for b in range(blocks)
    ]
    hots = [jnp.where(hit, 1.0, 0.0).astype(BF16) for hit in hits]
    counts = mm(jnp.concatenate(hots, axis=0), prefix_matrix())

    def place(boxes_ref, pos_ref, start, blocks, cap, wide):
        carry = jnp.zeros((DEV, 128), F32)
        parts = []
        for b in range(blocks):
            lanes = slice(b * 128, (b + 1) * 128)
            count = counts[(start + b) * 128:(start + b + 1) * 128]
            seen = count[:, :128] + carry
            pos = jnp.sum(jnp.where(hits[start + b], seen, 0.0), axis=0, keepdims=True) - 1.0
            carry = carry + count[:, 128:]
            pos = pos.astype(I32)
            pos_ref[:, lanes] = pos
            slot = boxes_ref[1:2, lanes]
            here = lax.broadcasted_iota(I32, (cap, 128), 0) == pos
            low = jnp.where(here, (slot & 255).astype(F32), 0.0)
            if wide:
                high = jnp.where(here, (slot >> 8).astype(F32), 0.0)
                low = jnp.concatenate([low, high], axis=0)
            parts.append(low.astype(BF16))
        table = mm_nt(
            jnp.concatenate(parts, axis=1), jnp.concatenate(hots[start:start + blocks], axis=1)
        )
        if wide:
            table = table[:cap] + 256.0 * table[cap:]
        return table

    fine = place(f_boxes, f_pos, 0, f_blocks, CAP_F, True)
    coarse = place(c_boxes, c_pos, f_blocks, c_blocks, CAP_C, False)
    rest = jnp.zeros((128 - CAP_F - CAP_C, DEV), F32)
    table = jnp.concatenate([fine, coarse, rest], axis=0)
    slots_ref[:, 0, :] = jnp.transpose(table).astype(I32)


def operator_copies(ops_in, ops, sems):
    each = RANK // OPS_CHUNKS
    return [
        pltpu.make_async_copy(
            ops_in.at[pl.ds(k * each, each)], ops.at[pl.ds(k * each, each)], sems.at[k]
        )
        for k in range(OPS_CHUNKS)
    ]


def pick_operators(copies, ops, kinds, flat, out):
    groups, nt = kinds.shape[0], ops.shape[2]
    hot = jnp.where(kinds[:, 0:1] == lax.broadcasted_iota(I32, (groups, nt), 1), 1.0, 0.0)
    hot = hot.astype(BF16)
    for quad in range(RANK // 4):
        if quad % (RANK // 4 // OPS_CHUNKS) == 0:
            copies[quad // (RANK // 4 // OPS_CHUNKS)].wait()
        rows = ops[quad * 4:(quad + 1) * 4].reshape(256, nt)
        got = mm_nt(hot, rows)
        for k in range(4):
            flat[pl.ds(quad * 4 + k, groups, stride=RANK), :] = got[:, k * RANK:(k + 1) * RANK]
    out[...] = flat[...].reshape(groups, RANK, RANK).astype(BF16)


def outgoing_kernel(
    ops_in, s_ff, s_fc, fm, cm, f_owner, f_boxes, f_pos, c_owner, c_boxes, c_pos,
    sel_ref, f_part, c_part, ops, f_vec, c_vec, kinds, kf, pm, hot_out, flat, sems,
):
    copies = operator_copies(ops_in, ops, sems)
    for copy in copies:
        copy.start()
    row = f_boxes[0:1, :]
    f_vec[...] = pick_fine(half_stack(fm[...]), one_hot(row & 255, 256), row).astype(BF16)
    c_vec[...] = mm(cm[...], one_hot(c_boxes[0:1, :], 64)).astype(BF16)
    pos = f_pos[...]
    hot_out[...] = one_hot((pos >> 4) * DEV + f_owner[...], 2 * DEV)
    kinds[...] = jnp.zeros_like(kinds)
    kinds[0:G_FAR_F] = s_ff[...]
    kinds[G_FAR_F:G_FAR_F + G_FAR_C] = s_fc[...]
    pick_operators(copies, ops, kinds, kf, sel_ref)

    part = jnp.concatenate(
        [
            mm_tn(sel_ref[G_FAR_F + g], c_vec[:, g * 128:(g + 1) * 128])
            for g in range(G_FAR_C)
        ],
        axis=1,
    )
    at = c_pos[...]
    pieces = [jnp.where(at == k, part, 0.0).astype(BF16) for k in range(CAP_C)]
    big = mm_nt(jnp.concatenate(pieces, axis=0), one_hot(c_owner[...], DEV))
    for kp in range(ROWS_C):
        c_part[kp] = jnp.transpose(big[kp * 128:(kp + 1) * 128])

    part = jnp.concatenate(
        [mm_tn(sel_ref[g], f_vec[:, g * 128:(g + 1) * 128]) for g in range(G_FAR_F)], axis=1
    )
    part = (2.0 * part).astype(BF16)
    step = jnp.broadcast_to((pos & (HALF_CAP - 1)).astype(BF16), part.shape)
    none = jnp.zeros((), BF16)
    for k in range(HALF_CAP):
        pm[k * RANK:(k + 1) * RANK, :] = jnp.where(step == jnp.asarray(k, BF16), part, none)
    for j in range(HALF_CAP * RANK // PM_ROWS):
        big = mm_nt(pm[j * PM_ROWS:(j + 1) * PM_ROWS, :], hot_out[...])
        for i in range(PM_ROWS // 128):
            kp = j * (PM_ROWS // 128) + i
            for half in range(2):
                turned = jnp.transpose(big[i * 128:(i + 1) * 128, half * DEV:(half + 1) * DEV])
                flat[pl.ds(half * (HALF_CAP // 2) + kp, DEV, stride=ROWS_F), :] = turned

    f_part[...] = flat[...].reshape(DEV, ROWS_F, 128).astype(BF16)


def slot_rows(slots):
    table = jnp.transpose(slots[:, 0, :].astype(F32)).astype(I32)
    rows = [table[k:k + 1] for k in range(CAP_F + CAP_C)]
    return jnp.concatenate(rows[:CAP_F], axis=1), jnp.concatenate(rows[CAP_F:], axis=1)


def reply_kernel(slots, fm, cm, f_part, c_part, out_ref, f_flat, c_flat):
    f_row, c_row = slot_rows(slots)
    f_vec = pick_fine(half_stack(fm[...]), one_hot(f_row & 255, 256), f_row)
    c_vec = mm(cm[...], one_hot(c_row, 64))

    def turned(vec, kp):
        at = 2 * kp * DEV
        return jnp.transpose(
            jnp.concatenate([vec[:, at:at + DEV], vec[:, at + DEV:at + 2 * DEV]], axis=0)
        )

    for kp in range(ROWS_F):
        f_flat[pl.ds(kp, DEV, stride=ROWS_F), :] = turned(f_vec, kp)
    for kp in range(ROWS_C):
        c_flat[pl.ds(kp, DEV, stride=2 * ROWS_C), :] = turned(c_vec, kp)
        c_flat[pl.ds(ROWS_C + kp, DEV, stride=2 * ROWS_C), :] = c_part[kp]
    out_ref[...] = jnp.concatenate(
        [
            f_flat[...].reshape(DEV, ROWS_F, 128).astype(BF16),
            f_part[...],
            c_flat[...].reshape(DEV, 2 * ROWS_C, 128).astype(BF16),
        ],
        axis=1,
    )


def near_kernel(
    ops_in, s_nf, s_nc, fm, cm, f_boxes, c_boxes, f_out, c_out, ops, kinds, kf, sel, f_sum, sems
):
    copies = operator_copies(ops_in, ops, sems)
    for copy in copies:
        copy.start()
    kinds[0:G_NEAR_F] = s_nf[...]
    kinds[G_NEAR_F:NEAR_GROUPS] = s_nc[...]
    pick_operators(copies, ops, kinds, kf, sel)
    stack = half_stack(fm[...])
    f_sum[...] = jnp.zeros_like(f_sum)

    def step(i, carry):
        lanes = pl.ds(pl.multiple_of(i * NEAR_BLOCK, NEAR_BLOCK), NEAR_BLOCK)
        first = f_boxes[0:1, lanes]
        second = f_boxes[1:2, lanes]
        hot_1 = one_hot(first & 255, 256)
        hot_2 = one_hot(second & 255, 256)
        vec_1 = pick_fine(stack, hot_1, first).astype(BF16)
        vec_2 = pick_fine(stack, hot_2, second).astype(BF16)
        to_1, to_2 = [], []
        for k in range(NEAR_BLOCK // 128):
            op = sel[NEAR_BLOCK // 128 * i + k]
            cut = slice(k * 128, (k + 1) * 128)
            to_1.append(mm(op, vec_2[:, cut]))
            to_2.append(mm_tn(op, vec_1[:, cut]))
        to_1 = jnp.concatenate(to_1, axis=1)
        to_2 = jnp.concatenate(to_2, axis=1)
        both = jnp.concatenate([spread_fine(to_1, first), spread_fine(to_2, second)], axis=1)
        hots = jnp.concatenate([hot_1, hot_2], axis=1)
        f_sum[...] += mm_nt(both, hots)
        return carry

    lax.fori_loop(0, G_NEAR_F * 128 // NEAR_BLOCK, step, 0)
    f_out[...] = f_sum[:2 * RANK] + f_sum[2 * RANK:]
    total = jnp.zeros((2 * RANK, 64), F32)
    for g in range(G_NEAR_C):
        lanes = slice(g * 128, (g + 1) * 128)
        hot_1 = one_hot(c_boxes[0:1, lanes], 64)
        hot_2 = one_hot(c_boxes[1:2, lanes], 64)
        vec_1 = mm(cm[...], hot_1).astype(BF16)
        vec_2 = mm(cm[...], hot_2).astype(BF16)
        op = sel[G_NEAR_F + g]
        total = total + mm_nt(split_rows(mm(op, vec_2)), hot_1)
        total = total + mm_nt(split_rows(mm_tn(op, vec_1)), hot_2)
    c_out[...] = total[:RANK] + total[RANK:]


def final_kernel(
    got, slots, sel, f_near, c_near, parent, maps, f_owner, f_boxes, f_pos, c_owner, c_boxes, c_pos,
    c_ref, f_ref, flat,
):
    flat[...] = got[...].astype(F32).reshape(DEV * ROWS, 128)
    f_row, c_row = slot_rows(slots)

    def turned(row):
        return jnp.transpose(flat[pl.ds(row, DEV, stride=ROWS), :])

    def choose(found, where, count):
        vec = found[:RANK]
        for k in range(1, count):
            vec = jnp.where(where == k, found[k * RANK:(k + 1) * RANK], vec)
        return vec.astype(BF16)

    held_c = jnp.concatenate([turned(2 * ROWS_F + kp) for kp in range(ROWS_C)], axis=0)
    vec_c = choose(mm(held_c.astype(BF16), one_hot(c_owner[...], DEV)), c_pos[...], CAP_C)
    to_1 = jnp.concatenate(
        [mm(sel[G_FAR_F + g], vec_c[:, g * 128:(g + 1) * 128]) for g in range(G_FAR_C)], axis=1
    )
    far_c = mm_nt(split_rows(to_1), one_hot(c_boxes[0:1, :], 64))
    sides_c = []
    for kp in range(ROWS_C):
        arrived = turned(2 * ROWS_F + ROWS_C + kp)
        sides_c += [arrived[:RANK], arrived[RANK:]]
    arrived_c = mm_nt(jnp.concatenate(sides_c, axis=1).astype(BF16), one_hot(c_row, 64))
    coarse = parent[...] + c_near[...] + far_c[:RANK] + far_c[RANK:] + arrived_c
    coarse = coarse.astype(BF16)
    c_ref[...] = coarse

    held = jnp.concatenate(
        [
            jnp.concatenate([turned(quarter * (ROWS_F // 4) + kp) for quarter in range(4)], axis=1)
            for kp in range(ROWS_F // 4)
        ],
        axis=0,
    ).astype(BF16)
    pos = f_pos[...]
    hot = one_hot_wide((pos // PART_CAP) * DEV + f_owner[...], 4 * DEV)
    vec = choose(mm(held, hot), pos & (PART_CAP - 1), PART_CAP)
    to_1 = jnp.concatenate(
        [mm(sel[g], vec[:, g * 128:(g + 1) * 128]) for g in range(G_FAR_F)], axis=1
    )
    first = f_boxes[0:1, :]
    total = mm_nt(spread_fine(to_1, first), one_hot(first & 255, 256))
    sides = []
    for kp in range(ROWS_F):
        arrived = turned(ROWS_F + kp)
        sides += [arrived[:RANK], arrived[RANK:]]
    side = jnp.concatenate(sides, axis=1)
    side = jnp.concatenate(
        [jnp.where(f_row < 256, side, 0.0), jnp.where(f_row < 256, 0.0, side)], axis=0
    )
    added = mm_nt(side.astype(BF16), one_hot(f_row & 255, 256))

    box = lax.broadcasted_iota(I32, (64, 512), 1)
    parent_of = jnp.where((box >> 3) == lax.broadcasted_iota(I32, (64, 512), 0), 1.0, 0.0)
    wide = mm(coarse, parent_of.astype(BF16)).astype(BF16)
    starts = mm(maps[...].reshape(8 * RANK, RANK), wide)
    start = starts[:RANK]
    for k in range(1, 8):
        start = jnp.where((box & 7) == k, starts[k * RANK:(k + 1) * RANK], start)

    total = 2.0 * (f_near[...] + total[:2 * RANK] + total[2 * RANK:]) + added
    fine = start + jnp.concatenate([total[:RANK], total[RANK:]], axis=1)
    f_ref[...] = fine.astype(BF16)


def call(kernel, out_shape, scratch, mib, flops, nbytes, *args, **more):
    return pl.pallas_call(
        kernel,
        out_shape=out_shape,
        scratch_shapes=scratch,
        compiler_params=pltpu.CompilerParams(vmem_limit_bytes=mib * 1024 * 1024),
        cost_estimate=pl.CostEstimate(flops=flops, bytes_accessed=nbytes, transcendentals=0),
        **more,
    )(*args)


def on_device(
    coarse_multipole,
    fine_multipole,
    parent_local,
    operators,
    child_maps,
    coarse_near_boxes,
    coarse_near_shift,
    coarse_far_boxes,
    coarse_far_owner,
    coarse_far_shift,
    fine_near_boxes,
    fine_near_shift,
    fine_far_boxes,
    fine_far_owner,
    fine_far_shift,
):
    def sds(shape, dtype):
        return jax.ShapeDtypeStruct(shape, dtype)

    def in_hbm(x):
        return pltpu.with_memory_space_constraint(x, pltpu.HBM)

    fm, cm = fine_multipole, coarse_multipole
    vmem = pl.BlockSpec(memory_space=pltpu.VMEM)
    hbm = pl.BlockSpec(memory_space=pltpu.HBM)
    f_owner, c_owner = fine_far_owner.T, coarse_far_owner.T
    f_far, c_far = fine_far_boxes.T, coarse_far_boxes.T
    ops = in_hbm(jnp.transpose(operators, (1, 2, 0)))

    n_f, n_c = f_owner.shape[1], c_owner.shape[1]
    slots, f_pos, c_pos, f_owner, f_far, c_owner, c_far = call(
        route_kernel,
        (
            sds((DEV, 1, 128), I32),
            pltpu.VMEM((1, n_f), I32),
            pltpu.VMEM((1, n_c), I32),
            pltpu.VMEM((1, n_f), I32),
            pltpu.VMEM((2, n_f), I32),
            pltpu.VMEM((1, n_c), I32),
            pltpu.VMEM((2, n_c), I32),
        ),
        [pltpu.SemaphoreType.DMA((4,))],
        MIB_1,
        10**9,
        10**6,
        *[in_hbm(x) for x in (f_owner, f_far, c_owner, c_far)],
        in_specs=[hbm] * 4,
    )
    asked = lax.all_to_all(slots, ("oct", "box"), split_axis=0, concat_axis=0, tiled=True)
    sel, f_part, c_part = call(
        outgoing_kernel,
        (
            sds((FAR_GROUPS, RANK, RANK), BF16),
            sds((DEV, ROWS_F, 128), BF16),
            sds((ROWS_C, DEV, 128), F32),
        ),
        [
            pltpu.VMEM(ops.shape, BF16),
            pltpu.VMEM((RANK, n_f), BF16),
            pltpu.VMEM((RANK, n_c), BF16),
            pltpu.VMEM((FAR_GROUPS, 128), I32),
            pltpu.VMEM((FAR_GROUPS * RANK, RANK), F32),
            pltpu.VMEM((HALF_CAP * RANK, n_f), BF16),
            pltpu.VMEM((2 * DEV, n_f), BF16),
            pltpu.VMEM((DEV * ROWS_F, 128), F32),
            pltpu.SemaphoreType.DMA((OPS_CHUNKS,)),
        ],
        MIB_2,
        5 * 10**9,
        10**7,
        ops,
        fine_far_shift.reshape(-1, 128),
        coarse_far_shift.reshape(-1, 128),
        fm, cm, f_owner, f_far, f_pos, c_owner, c_far, c_pos,
        in_specs=[hbm] + [vmem] * 10,
    )
    sent = call(
        reply_kernel,
        sds((DEV, ROWS, 128), BF16),
        [pltpu.VMEM((DEV * ROWS_F, 128), F32), pltpu.VMEM((DEV * 2 * ROWS_C, 128), F32)],
        MIB_3,
        10**9,
        10**6,
        asked, fm, cm, f_part, c_part,
    )
    got = lax.all_to_all(sent, ("oct", "box"), split_axis=0, concat_axis=0, tiled=True)
    f_near, c_near = call(
        near_kernel,
        (sds((2 * RANK, 256), F32), sds((RANK, 64), F32)),
        [
            pltpu.VMEM(ops.shape, BF16),
            pltpu.VMEM((NEAR_GROUPS, 128), I32),
            pltpu.VMEM((NEAR_GROUPS * RANK, RANK), F32),
            pltpu.VMEM((NEAR_GROUPS, RANK, RANK), BF16),
            pltpu.VMEM((4 * RANK, 256), F32),
            pltpu.SemaphoreType.DMA((OPS_CHUNKS,)),
        ],
        MIB_4,
        10**10,
        10**7,
        ops,
        fine_near_shift.reshape(-1, 128),
        coarse_near_shift.reshape(-1, 128),
        fm, cm, fine_near_boxes.T, coarse_near_boxes.T,
        in_specs=[hbm] + [vmem] * 6,
    )
    return call(
        final_kernel,
        (sds((RANK, 64), BF16), sds((RANK, 512), BF16)),
        [pltpu.VMEM((DEV * ROWS, 128), F32)],
        MIB_5,
        3 * 10**9,
        10**7,
        got, asked, sel, f_near, c_near, parent_local, child_maps,
        f_owner, f_far, f_pos, c_owner, c_far, c_pos,
    )


def solution(mesh):
    both = ("oct", "box")
    return jax.shard_map(
        on_device,
        mesh=mesh,
        in_specs=(
            P(None, both),
            P(None, both),
            P(None, both),
            P(),
            P(),
            P(both, None),
            P(both),
            P(both, None),
            P(both, None),
            P(both),
            P(both, None),
            P(both),
            P(both, None),
            P(both, None),
            P(both),
        ),
        out_specs=(P(None, both), P(None, both)),
        check_vma=False,
    )
```

```python
import jax
import jax.numpy as jnp
from jax import lax
from jax.experimental import pallas as pl
from jax.experimental.pallas import tpu as pltpu
from jax.sharding import PartitionSpec as P


F32 = jnp.float32
BF16 = jnp.bfloat16
I32 = jnp.int32

DEV = 128
RANK = 64
CAP_F = 32
CAP_C = 8
ROWS_F = CAP_F * RANK // 128
ROWS_C = CAP_C * RANK // 128
ROWS = 2 * (ROWS_F + ROWS_C)
HALF_CAP = CAP_F // 2
PART_CAP = CAP_F // 4
G_NEAR_F, G_FAR_F, G_NEAR_C, G_FAR_C = 64, 16, 8, 4
FAR_GROUPS = 24
NEAR_GROUPS = G_NEAR_F + G_NEAR_C
NEAR_BLOCK = 4096
PM_ROWS = 512
OPS_CHUNKS = 2
MIB_1, MIB_2, MIB_3, MIB_4, MIB_5 = 16, 36, 24, 44, 40


def mm(a, b):
    return lax.dot_general(a, b, (((1,), (0,)), ((), ())), preferred_element_type=F32)


def mm_nt(a, b):
    return lax.dot_general(a, b, (((1,), (1,)), ((), ())), preferred_element_type=F32)


def mm_tn(a, b):
    return lax.dot_general(a, b, (((0,), (0,)), ((), ())), preferred_element_type=F32)


def one_hot(row, count):
    n = row.shape[1]
    at = lax.broadcasted_iota(I32, (count, n), 0).astype(BF16)
    hit = at == jnp.broadcast_to(row.astype(BF16), (count, n))
    return jnp.where(hit, jnp.ones((), BF16), jnp.zeros((), BF16))


def one_hot_wide(row, count):
    return jnp.concatenate(
        [one_hot(jnp.clip(row - at, -1, 256), 256) for at in range(0, count, 256)], axis=0
    )


def half_stack(m):
    return jnp.concatenate([m[:, :256], m[:, 256:]], axis=0)


def pick_fine(stack, hot, row):
    both = mm(stack, hot)
    return jnp.where(row < 256, both[:RANK], both[RANK:])


def split_rows(values):
    high = values.astype(BF16)
    low = (values - high.astype(F32)).astype(BF16)
    return jnp.concatenate([high, low], axis=0)


def spread_fine(values, row):
    first = jnp.where(row < 256, values, 0.0)
    second = jnp.where(row < 256, 0.0, values)
    return split_rows(jnp.concatenate([first, second], axis=0))


def prefix_matrix():
    down = lax.broadcasted_iota(I32, (128, 256), 0)
    across = lax.broadcasted_iota(I32, (128, 256), 1)
    return jnp.where((down <= across) | (across >= 128), 1.0, 0.0).astype(BF16)


def route_kernel(
    f_owner_in, f_boxes_in, c_owner_in, c_boxes_in,
    slots_ref, f_pos, c_pos, f_owner, f_boxes, c_owner, c_boxes, sems,
):
    copies = [
        pltpu.make_async_copy(source, target, sems.at[i])
        for i, (source, target) in enumerate(
            [
                (f_owner_in, f_owner),
                (c_owner_in, c_owner),
                (f_boxes_in, f_boxes),
                (c_boxes_in, c_boxes),
            ]
        )
    ]
    for copy in copies:
        copy.start()
    for copy in copies:
        copy.wait()
    f_blocks, c_blocks = f_owner.shape[1] // 128, c_owner.shape[1] // 128
    hits = [
        lax.broadcasted_iota(I32, (DEV, 128), 0) == ref[:, b * 128:(b + 1) * 128]
        for ref, blocks in ((f_owner, f_blocks), (c_owner, c_blocks))
        for b in range(blocks)
    ]
    hots = [jnp.where(hit, 1.0, 0.0).astype(BF16) for hit in hits]
    counts = mm(jnp.concatenate(hots, axis=0), prefix_matrix())

    def place(boxes_ref, pos_ref, start, blocks, cap, wide):
        carry = jnp.zeros((DEV, 128), F32)
        parts = []
        for b in range(blocks):
            lanes = slice(b * 128, (b + 1) * 128)
            count = counts[(start + b) * 128:(start + b + 1) * 128]
            seen = count[:, :128] + carry
            pos = jnp.sum(jnp.where(hits[start + b], seen, 0.0), axis=0, keepdims=True) - 1.0
            carry = carry + count[:, 128:]
            pos = pos.astype(I32)
            pos_ref[:, lanes] = pos
            slot = boxes_ref[1:2, lanes]
            here = lax.broadcasted_iota(I32, (cap, 128), 0) == pos
            low = jnp.where(here, (slot & 255).astype(F32), 0.0)
            if wide:
                high = jnp.where(here, (slot >> 8).astype(F32), 0.0)
                low = jnp.concatenate([low, high], axis=0)
            parts.append(low.astype(BF16))
        table = mm_nt(
            jnp.concatenate(parts, axis=1), jnp.concatenate(hots[start:start + blocks], axis=1)
        )
        if wide:
            table = table[:cap] + 256.0 * table[cap:]
        return table

    fine = place(f_boxes, f_pos, 0, f_blocks, CAP_F, True)
    coarse = place(c_boxes, c_pos, f_blocks, c_blocks, CAP_C, False)
    rest = jnp.zeros((128 - CAP_F - CAP_C, DEV), F32)
    table = jnp.concatenate([fine, coarse, rest], axis=0)
    slots_ref[:, 0, :] = jnp.transpose(table).astype(I32)


def operator_copies(ops_in, ops, sems):
    each = RANK // OPS_CHUNKS
    return [
        pltpu.make_async_copy(
            ops_in.at[pl.ds(k * each, each)], ops.at[pl.ds(k * each, each)], sems.at[k]
        )
        for k in range(OPS_CHUNKS)
    ]


def pick_operators(copies, ops, kinds, flat, out):
    groups, nt = kinds.shape[0], ops.shape[2]
    hot = jnp.where(kinds[:, 0:1] == lax.broadcasted_iota(I32, (groups, nt), 1), 1.0, 0.0)
    hot = hot.astype(BF16)
    for quad in range(RANK // 4):
        if quad % (RANK // 4 // OPS_CHUNKS) == 0:
            copies[quad // (RANK // 4 // OPS_CHUNKS)].wait()
        rows = ops[quad * 4:(quad + 1) * 4].reshape(256, nt)
        got = mm_nt(hot, rows)
        for k in range(4):
            flat[pl.ds(quad * 4 + k, groups, stride=RANK), :] = got[:, k * RANK:(k + 1) * RANK]
    out[...] = flat[...].reshape(groups, RANK, RANK).astype(BF16)


def outgoing_kernel(
    ops_in, s_ff, s_fc, fm, cm, f_owner, f_boxes, f_pos, c_owner, c_boxes, c_pos,
    sel_ref, f_part, c_part, ops, f_vec, c_vec, kinds, kf, pm, hot_out, flat, sems,
):
    copies = operator_copies(ops_in, ops, sems)
    for copy in copies:
        copy.start()
    row = f_boxes[0:1, :]
    f_vec[...] = pick_fine(half_stack(fm[...]), one_hot(row & 255, 256), row).astype(BF16)
    c_vec[...] = mm(cm[...], one_hot(c_boxes[0:1, :], 64)).astype(BF16)
    pos = f_pos[...]
    hot_out[...] = one_hot((pos >> 4) * DEV + f_owner[...], 2 * DEV)
    kinds[...] = jnp.zeros_like(kinds)
    kinds[0:G_FAR_F] = s_ff[...]
    kinds[G_FAR_F:G_FAR_F + G_FAR_C] = s_fc[...]
    pick_operators(copies, ops, kinds, kf, sel_ref)

    part = jnp.concatenate(
        [
            mm_tn(sel_ref[G_FAR_F + g], c_vec[:, g * 128:(g + 1) * 128])
            for g in range(G_FAR_C)
        ],
        axis=1,
    )
    at = c_pos[...]
    pieces = [jnp.where(at == k, part, 0.0).astype(BF16) for k in range(CAP_C)]
    big = mm_nt(jnp.concatenate(pieces, axis=0), one_hot(c_owner[...], DEV))
    for kp in range(ROWS_C):
        c_part[kp] = jnp.transpose(big[kp * 128:(kp + 1) * 128])

    part = jnp.concatenate(
        [mm_tn(sel_ref[g], f_vec[:, g * 128:(g + 1) * 128]) for g in range(G_FAR_F)], axis=1
    )
    part = (2.0 * part).astype(BF16)
    step = jnp.broadcast_to((pos & (HALF_CAP - 1)).astype(BF16), part.shape)
    none = jnp.zeros((), BF16)
    for k in range(HALF_CAP):
        pm[k * RANK:(k + 1) * RANK, :] = jnp.where(step == jnp.asarray(k, BF16), part, none)
    for j in range(HALF_CAP * RANK // PM_ROWS):
        big = mm_nt(pm[j * PM_ROWS:(j + 1) * PM_ROWS, :], hot_out[...])
        for i in range(PM_ROWS // 128):
            kp = j * (PM_ROWS // 128) + i
            for half in range(2):
                turned = jnp.transpose(big[i * 128:(i + 1) * 128, half * DEV:(half + 1) * DEV])
                flat[pl.ds(half * (HALF_CAP // 2) + kp, DEV, stride=ROWS_F), :] = turned

    f_part[...] = flat[...].reshape(DEV, ROWS_F, 128).astype(BF16)


def slot_rows(slots):
    table = jnp.transpose(slots[:, 0, :].astype(F32)).astype(I32)
    rows = [table[k:k + 1] for k in range(CAP_F + CAP_C)]
    return jnp.concatenate(rows[:CAP_F], axis=1), jnp.concatenate(rows[CAP_F:], axis=1)


def reply_kernel(slots, fm, cm, f_part, c_part, out_ref, f_flat, c_flat):
    f_row, c_row = slot_rows(slots)
    f_vec = pick_fine(half_stack(fm[...]), one_hot(f_row & 255, 256), f_row)
    c_vec = mm(cm[...], one_hot(c_row, 64))

    def turned(vec, kp):
        at = 2 * kp * DEV
        return jnp.transpose(
            jnp.concatenate([vec[:, at:at + DEV], vec[:, at + DEV:at + 2 * DEV]], axis=0)
        )

    for kp in range(ROWS_F):
        f_flat[pl.ds(kp, DEV, stride=ROWS_F), :] = turned(f_vec, kp)
    for kp in range(ROWS_C):
        c_flat[pl.ds(kp, DEV, stride=2 * ROWS_C), :] = turned(c_vec, kp)
        c_flat[pl.ds(ROWS_C + kp, DEV, stride=2 * ROWS_C), :] = c_part[kp]
    out_ref[...] = jnp.concatenate(
        [
            f_flat[...].reshape(DEV, ROWS_F, 128).astype(BF16),
            f_part[...],
            c_flat[...].reshape(DEV, 2 * ROWS_C, 128).astype(BF16),
        ],
        axis=1,
    )


def near_kernel(
    ops_in, s_nf, s_nc, fm, cm, f_boxes, c_boxes, slots, f_owner, f_far, f_pos,
    f_out, c_out, hot_owner, hot_first, hot_slot, ops, kinds, kf, sel, f_sum, sems,
):
    copies = operator_copies(ops_in, ops, sems)
    for copy in copies:
        copy.start()
    hot_owner[...] = one_hot_wide((f_pos[...] // PART_CAP) * DEV + f_owner[...], 4 * DEV)
    hot_first[...] = jnp.transpose(one_hot(f_far[0:1, :] & 255, 256))
    hot_slot[...] = jnp.transpose(one_hot(slot_rows(slots)[0] & 255, 256))
    kinds[0:G_NEAR_F] = s_nf[...]
    kinds[G_NEAR_F:NEAR_GROUPS] = s_nc[...]
    pick_operators(copies, ops, kinds, kf, sel)
    stack = half_stack(fm[...])
    f_sum[...] = jnp.zeros_like(f_sum)

    def step(i, carry):
        lanes = pl.ds(pl.multiple_of(i * NEAR_BLOCK, NEAR_BLOCK), NEAR_BLOCK)
        first = f_boxes[0:1, lanes]
        second = f_boxes[1:2, lanes]
        hot_1 = one_hot(first & 255, 256)
        hot_2 = one_hot(second & 255, 256)
        vec_1 = pick_fine(stack, hot_1, first).astype(BF16)
        vec_2 = pick_fine(stack, hot_2, second).astype(BF16)
        to_1, to_2 = [], []
        for k in range(NEAR_BLOCK // 128):
            op = sel[NEAR_BLOCK // 128 * i + k]
            cut = slice(k * 128, (k + 1) * 128)
            to_1.append(mm(op, vec_2[:, cut]))
            to_2.append(mm_tn(op, vec_1[:, cut]))
        to_1 = jnp.concatenate(to_1, axis=1)
        to_2 = jnp.concatenate(to_2, axis=1)
        both = jnp.concatenate([spread_fine(to_1, first), spread_fine(to_2, second)], axis=1)
        hots = jnp.concatenate([hot_1, hot_2], axis=1)
        f_sum[...] += mm_nt(both, hots)
        return carry

    lax.fori_loop(0, G_NEAR_F * 128 // NEAR_BLOCK, step, 0)
    f_out[...] = f_sum[:2 * RANK] + f_sum[2 * RANK:]
    total = jnp.zeros((2 * RANK, 64), F32)
    for g in range(G_NEAR_C):
        lanes = slice(g * 128, (g + 1) * 128)
        hot_1 = one_hot(c_boxes[0:1, lanes], 64)
        hot_2 = one_hot(c_boxes[1:2, lanes], 64)
        vec_1 = mm(cm[...], hot_1).astype(BF16)
        vec_2 = mm(cm[...], hot_2).astype(BF16)
        op = sel[G_NEAR_F + g]
        total = total + mm_nt(split_rows(mm(op, vec_2)), hot_1)
        total = total + mm_nt(split_rows(mm_tn(op, vec_1)), hot_2)
    c_out[...] = total[:RANK] + total[RANK:]


def final_kernel(
    got, slots, sel, f_near, c_near, hot_owner, hot_first, hot_slot, parent, maps, f_boxes, f_pos,
    c_owner, c_boxes, c_pos, c_ref, f_ref, flat,
):
    flat[...] = got[...].astype(F32).reshape(DEV * ROWS, 128)
    f_row, c_row = slot_rows(slots)

    def turned(row):
        return jnp.transpose(flat[pl.ds(row, DEV, stride=ROWS), :])

    def choose(found, where, count):
        vec = found[:RANK]
        for k in range(1, count):
            vec = jnp.where(where == k, found[k * RANK:(k + 1) * RANK], vec)
        return vec.astype(BF16)

    held_c = jnp.concatenate([turned(2 * ROWS_F + kp) for kp in range(ROWS_C)], axis=0)
    vec_c = choose(mm(held_c.astype(BF16), one_hot(c_owner[...], DEV)), c_pos[...], CAP_C)
    to_1 = jnp.concatenate(
        [mm(sel[G_FAR_F + g], vec_c[:, g * 128:(g + 1) * 128]) for g in range(G_FAR_C)], axis=1
    )
    far_c = mm_nt(split_rows(to_1), one_hot(c_boxes[0:1, :], 64))
    sides_c = []
    for kp in range(ROWS_C):
        arrived = turned(2 * ROWS_F + ROWS_C + kp)
        sides_c += [arrived[:RANK], arrived[RANK:]]
    arrived_c = mm_nt(jnp.concatenate(sides_c, axis=1).astype(BF16), one_hot(c_row, 64))
    coarse = parent[...] + c_near[...] + far_c[:RANK] + far_c[RANK:] + arrived_c
    coarse = coarse.astype(BF16)
    c_ref[...] = coarse

    held = jnp.concatenate(
        [
            jnp.concatenate([turned(quarter * (ROWS_F // 4) + kp) for quarter in range(4)], axis=1)
            for kp in range(ROWS_F // 4)
        ],
        axis=0,
    ).astype(BF16)
    pos = f_pos[...]
    vec = choose(mm(held, hot_owner[...]), pos & (PART_CAP - 1), PART_CAP)
    to_1 = jnp.concatenate(
        [mm(sel[g], vec[:, g * 128:(g + 1) * 128]) for g in range(G_FAR_F)], axis=1
    )
    first = f_boxes[0:1, :]
    total = mm(spread_fine(to_1, first), hot_first[...])
    sides = []
    for kp in range(ROWS_F):
        arrived = turned(ROWS_F + kp)
        sides += [arrived[:RANK], arrived[RANK:]]
    side = jnp.concatenate(sides, axis=1)
    side = jnp.concatenate(
        [jnp.where(f_row < 256, side, 0.0), jnp.where(f_row < 256, 0.0, side)], axis=0
    )
    added = mm(side.astype(BF16), hot_slot[...])

    box = lax.broadcasted_iota(I32, (64, 512), 1)
    parent_of = jnp.where((box >> 3) == lax.broadcasted_iota(I32, (64, 512), 0), 1.0, 0.0)
    wide = mm(coarse, parent_of.astype(BF16)).astype(BF16)
    starts = mm(maps[...].reshape(8 * RANK, RANK), wide)
    start = starts[:RANK]
    for k in range(1, 8):
        start = jnp.where((box & 7) == k, starts[k * RANK:(k + 1) * RANK], start)

    total = 2.0 * (f_near[...] + total[:2 * RANK] + total[2 * RANK:]) + added
    fine = start + jnp.concatenate([total[:RANK], total[RANK:]], axis=1)
    f_ref[...] = fine.astype(BF16)


def call(kernel, out_shape, scratch, mib, flops, nbytes, *args, **more):
    return pl.pallas_call(
        kernel,
        out_shape=out_shape,
        scratch_shapes=scratch,
        compiler_params=pltpu.CompilerParams(vmem_limit_bytes=mib * 1024 * 1024),
        cost_estimate=pl.CostEstimate(flops=flops, bytes_accessed=nbytes, transcendentals=0),
        **more,
    )(*args)


def on_device(
    coarse_multipole,
    fine_multipole,
    parent_local,
    operators,
    child_maps,
    coarse_near_boxes,
    coarse_near_shift,
    coarse_far_boxes,
    coarse_far_owner,
    coarse_far_shift,
    fine_near_boxes,
    fine_near_shift,
    fine_far_boxes,
    fine_far_owner,
    fine_far_shift,
):
    def sds(shape, dtype):
        return jax.ShapeDtypeStruct(shape, dtype)

    def in_hbm(x):
        return pltpu.with_memory_space_constraint(x, pltpu.HBM)

    fm, cm = fine_multipole, coarse_multipole
    vmem = pl.BlockSpec(memory_space=pltpu.VMEM)
    hbm = pl.BlockSpec(memory_space=pltpu.HBM)
    f_owner, c_owner = fine_far_owner.T, coarse_far_owner.T
    f_far, c_far = fine_far_boxes.T, coarse_far_boxes.T
    ops = in_hbm(jnp.transpose(operators, (1, 2, 0)))

    n_f, n_c = f_owner.shape[1], c_owner.shape[1]
    slots, f_pos, c_pos, f_owner, f_far, c_owner, c_far = call(
        route_kernel,
        (
            sds((DEV, 1, 128), I32),
            pltpu.VMEM((1, n_f), I32),
            pltpu.VMEM((1, n_c), I32),
            pltpu.VMEM((1, n_f), I32),
            pltpu.VMEM((2, n_f), I32),
            pltpu.VMEM((1, n_c), I32),
            pltpu.VMEM((2, n_c), I32),
        ),
        [pltpu.SemaphoreType.DMA((4,))],
        MIB_1,
        10**9,
        10**6,
        *[in_hbm(x) for x in (f_owner, f_far, c_owner, c_far)],
        in_specs=[hbm] * 4,
    )
    asked = lax.all_to_all(slots, ("oct", "box"), split_axis=0, concat_axis=0, tiled=True)
    sel, f_part, c_part = call(
        outgoing_kernel,
        (
            sds((FAR_GROUPS, RANK, RANK), BF16),
            sds((DEV, ROWS_F, 128), BF16),
            sds((ROWS_C, DEV, 128), F32),
        ),
        [
            pltpu.VMEM(ops.shape, BF16),
            pltpu.VMEM((RANK, n_f), BF16),
            pltpu.VMEM((RANK, n_c), BF16),
            pltpu.VMEM((FAR_GROUPS, 128), I32),
            pltpu.VMEM((FAR_GROUPS * RANK, RANK), F32),
            pltpu.VMEM((HALF_CAP * RANK, n_f), BF16),
            pltpu.VMEM((2 * DEV, n_f), BF16),
            pltpu.VMEM((DEV * ROWS_F, 128), F32),
            pltpu.SemaphoreType.DMA((OPS_CHUNKS,)),
        ],
        MIB_2,
        5 * 10**9,
        10**7,
        ops,
        fine_far_shift.reshape(-1, 128),
        coarse_far_shift.reshape(-1, 128),
        fm, cm, f_owner, f_far, f_pos, c_owner, c_far, c_pos,
        in_specs=[hbm] + [vmem] * 10,
    )
    sent = call(
        reply_kernel,
        sds((DEV, ROWS, 128), BF16),
        [pltpu.VMEM((DEV * ROWS_F, 128), F32), pltpu.VMEM((DEV * 2 * ROWS_C, 128), F32)],
        MIB_3,
        10**9,
        10**6,
        asked, fm, cm, f_part, c_part,
    )
    got = lax.all_to_all(sent, ("oct", "box"), split_axis=0, concat_axis=0, tiled=True)
    f_near, c_near, hot_owner, hot_first, hot_slot = call(
        near_kernel,
        (
            pltpu.VMEM((2 * RANK, 256), F32),
            pltpu.VMEM((RANK, 64), F32),
            pltpu.VMEM((4 * DEV, n_f), BF16),
            pltpu.VMEM((n_f, 256), BF16),
            pltpu.VMEM((CAP_F * DEV, 256), BF16),
        ),
        [
            pltpu.VMEM(ops.shape, BF16),
            pltpu.VMEM((NEAR_GROUPS, 128), I32),
            pltpu.VMEM((NEAR_GROUPS * RANK, RANK), F32),
            pltpu.VMEM((NEAR_GROUPS, RANK, RANK), BF16),
            pltpu.VMEM((4 * RANK, 256), F32),
            pltpu.SemaphoreType.DMA((OPS_CHUNKS,)),
        ],
        MIB_4,
        10**10,
        10**7,
        ops,
        fine_near_shift.reshape(-1, 128),
        coarse_near_shift.reshape(-1, 128),
        fm, cm, fine_near_boxes.T, coarse_near_boxes.T, asked, f_owner, f_far, f_pos,
        in_specs=[hbm] + [vmem] * 10,
    )
    return call(
        final_kernel,
        (sds((RANK, 64), BF16), sds((RANK, 512), BF16)),
        [pltpu.VMEM((DEV * ROWS, 128), F32)],
        MIB_5,
        3 * 10**9,
        10**7,
        got, asked, sel, f_near, c_near, hot_owner, hot_first, hot_slot, parent_local, child_maps,
        f_far, f_pos, c_owner, c_far, c_pos,
    )


def solution(mesh):
    both = ("oct", "box")
    return jax.shard_map(
        on_device,
        mesh=mesh,
        in_specs=(
            P(None, both),
            P(None, both),
            P(None, both),
            P(),
            P(),
            P(both, None),
            P(both),
            P(both, None),
            P(both, None),
            P(both),
            P(both, None),
            P(both),
            P(both, None),
            P(both, None),
            P(both),
        ),
        out_specs=(P(None, both), P(None, both)),
        check_vma=False,
    )
```

```python
import jax
import jax.numpy as jnp
from jax import lax
from jax.experimental import pallas as pl
from jax.experimental.pallas import tpu as pltpu
from jax.sharding import PartitionSpec as P


F32 = jnp.float32
BF16 = jnp.bfloat16
I32 = jnp.int32

DEV = 128
RANK = 64
CAP_F = 32
CAP_C = 8
ROWS_F = CAP_F * RANK // 128
ROWS_C = CAP_C * RANK // 128
ROWS = 2 * (ROWS_F + ROWS_C)
HALF_CAP = CAP_F // 2
PART_CAP = CAP_F // 4
G_NEAR_F, G_FAR_F, G_NEAR_C, G_FAR_C = 64, 16, 8, 4
FAR_GROUPS = 24
NEAR_GROUPS = G_NEAR_F + G_NEAR_C
NEAR_BLOCK = 4096
PM_ROWS = 512
OPS_CHUNKS = 2
SENDS = 4
MIB_1, MIB_2, MIB_3, MIB_4, MIB_5 = 16, 36, 24, 44, 40


def mm(a, b):
    return lax.dot_general(a, b, (((1,), (0,)), ((), ())), preferred_element_type=F32)


def mm_nt(a, b):
    return lax.dot_general(a, b, (((1,), (1,)), ((), ())), preferred_element_type=F32)


def mm_tn(a, b):
    return lax.dot_general(a, b, (((0,), (0,)), ((), ())), preferred_element_type=F32)


def one_hot(row, count):
    n = row.shape[1]
    at = lax.broadcasted_iota(I32, (count, n), 0).astype(BF16)
    hit = at == jnp.broadcast_to(row.astype(BF16), (count, n))
    return jnp.where(hit, jnp.ones((), BF16), jnp.zeros((), BF16))


def one_hot_wide(row, count):
    return jnp.concatenate(
        [one_hot(jnp.clip(row - at, -1, 256), 256) for at in range(0, count, 256)], axis=0
    )


def half_stack(m):
    return jnp.concatenate([m[:, :256], m[:, 256:]], axis=0)


def pick_fine(stack, hot, row):
    both = mm(stack, hot)
    return jnp.where(row < 256, both[:RANK], both[RANK:])


def split_rows(values):
    high = values.astype(BF16)
    low = (values - high.astype(F32)).astype(BF16)
    return jnp.concatenate([high, low], axis=0)


def spread_fine(values, row):
    first = jnp.where(row < 256, values, 0.0)
    second = jnp.where(row < 256, 0.0, values)
    return split_rows(jnp.concatenate([first, second], axis=0))


def prefix_matrix():
    down = lax.broadcasted_iota(I32, (128, 128), 0)
    across = lax.broadcasted_iota(I32, (128, 128), 1)
    return jnp.where(down <= across, 1.0, 0.0).astype(BF16)


def route_kernel(
    f_owner_in, f_boxes_in, c_owner_in, c_boxes_in,
    slots_ref, f_pos, c_pos, f_owner, f_boxes, c_owner, c_boxes, sems,
):
    copies = [
        pltpu.make_async_copy(source, target, sems.at[i])
        for i, (source, target) in enumerate(
            [
                (f_owner_in, f_owner),
                (c_owner_in, c_owner),
                (f_boxes_in, f_boxes),
                (c_boxes_in, c_boxes),
            ]
        )
    ]
    for copy in copies:
        copy.start()
    for copy in copies:
        copy.wait()
    f_blocks, c_blocks = f_owner.shape[1] // 128, c_owner.shape[1] // 128
    hits = [
        lax.broadcasted_iota(I32, (DEV, 128), 0) == ref[:, b * 128:(b + 1) * 128]
        for ref, blocks in ((f_owner, f_blocks), (c_owner, c_blocks))
        for b in range(blocks)
    ]
    hots = [jnp.where(hit, 1.0, 0.0).astype(BF16) for hit in hits]
    counts = mm(jnp.concatenate(hots, axis=0), prefix_matrix())

    def place(boxes_ref, pos_ref, start, blocks, cap, wide):
        carry = jnp.zeros((DEV, 128), F32)
        parts = []
        for b in range(blocks):
            lanes = slice(b * 128, (b + 1) * 128)
            count = counts[(start + b) * 128:(start + b + 1) * 128]
            seen = count + carry
            pos = jnp.sum(jnp.where(hits[start + b], seen, 0.0), axis=0, keepdims=True) - 1.0
            carry = carry + jnp.broadcast_to(count[:, 127:128], (DEV, 128))
            pos = pos.astype(I32)
            pos_ref[:, lanes] = pos
            slot = boxes_ref[1:2, lanes]
            here = lax.broadcasted_iota(I32, (cap, 128), 0) == pos
            low = jnp.where(here, (slot & 255).astype(F32), 0.0)
            if wide:
                high = jnp.where(here, (slot >> 8).astype(F32), 0.0)
                low = jnp.concatenate([low, high], axis=0)
            parts.append(low.astype(BF16))
        table = mm_nt(
            jnp.concatenate(parts, axis=1), jnp.concatenate(hots[start:start + blocks], axis=1)
        )
        if wide:
            table = table[:cap] + 256.0 * table[cap:]
        return table

    fine = place(f_boxes, f_pos, 0, f_blocks, CAP_F, True)
    coarse = place(c_boxes, c_pos, f_blocks, c_blocks, CAP_C, False)
    rest = jnp.zeros((128 - CAP_F - CAP_C, DEV), F32)
    table = jnp.concatenate([fine, coarse, rest], axis=0)
    slots_ref[:, 0, :] = jnp.transpose(table).astype(I32)


def operator_copies(ops_in, ops, sems):
    each = RANK // OPS_CHUNKS
    return [
        pltpu.make_async_copy(
            ops_in.at[pl.ds(k * each, each)], ops.at[pl.ds(k * each, each)], sems.at[k]
        )
        for k in range(OPS_CHUNKS)
    ]


def pick_operators(copies, ops, kinds, flat, out):
    groups, nt = kinds.shape[0], ops.shape[2]
    hot = jnp.where(kinds[:, 0:1] == lax.broadcasted_iota(I32, (groups, nt), 1), 1.0, 0.0)
    hot = hot.astype(BF16)
    for quad in range(RANK // 4):
        if quad % (RANK // 4 // OPS_CHUNKS) == 0:
            copies[quad // (RANK // 4 // OPS_CHUNKS)].wait()
        rows = ops[quad * 4:(quad + 1) * 4].reshape(256, nt)
        got = mm_nt(hot, rows)
        for k in range(4):
            flat[pl.ds(quad * 4 + k, groups, stride=RANK), :] = got[:, k * RANK:(k + 1) * RANK]
    out[...] = flat[...].reshape(groups, RANK, RANK).astype(BF16)


def outgoing_kernel(
    ops_in, s_ff, s_fc, fm, cm, f_owner, f_boxes, f_pos, c_owner, c_boxes, c_pos,
    sel_ref, f_part, c_part, ops, f_vec, c_vec, kinds, kf, pm, hot_out, flat, sems,
):
    copies = operator_copies(ops_in, ops, sems)
    for copy in copies:
        copy.start()
    row = f_boxes[0:1, :]
    f_vec[...] = pick_fine(half_stack(fm[...]), one_hot(row & 255, 256), row).astype(BF16)
    c_vec[...] = mm(cm[...], one_hot(c_boxes[0:1, :], 64)).astype(BF16)
    pos = f_pos[...]
    hot_out[...] = one_hot((pos >> 4) * DEV + f_owner[...], 2 * DEV)
    kinds[...] = jnp.zeros_like(kinds)
    kinds[0:G_FAR_F] = s_ff[...]
    kinds[G_FAR_F:G_FAR_F + G_FAR_C] = s_fc[...]
    pick_operators(copies, ops, kinds, kf, sel_ref)

    part = jnp.concatenate(
        [
            mm_tn(sel_ref[G_FAR_F + g], c_vec[:, g * 128:(g + 1) * 128])
            for g in range(G_FAR_C)
        ],
        axis=1,
    )
    at = c_pos[...]
    pieces = [jnp.where(at == k, part, 0.0).astype(BF16) for k in range(CAP_C)]
    big = mm_nt(jnp.concatenate(pieces, axis=0), one_hot(c_owner[...], DEV))
    for kp in range(ROWS_C):
        c_part[kp] = jnp.transpose(big[kp * 128:(kp + 1) * 128])

    part = jnp.concatenate(
        [mm_tn(sel_ref[g], f_vec[:, g * 128:(g + 1) * 128]) for g in range(G_FAR_F)], axis=1
    )
    part = (2.0 * part).astype(BF16)
    step = jnp.broadcast_to((pos & (HALF_CAP - 1)).astype(BF16), part.shape)
    none = jnp.zeros((), BF16)
    for k in range(HALF_CAP):
        pm[k * RANK:(k + 1) * RANK, :] = jnp.where(step == jnp.asarray(k, BF16), part, none)
    for j in range(HALF_CAP * RANK // PM_ROWS):
        big = mm_nt(pm[j * PM_ROWS:(j + 1) * PM_ROWS, :], hot_out[...])
        for i in range(PM_ROWS // 128):
            kp = j * (PM_ROWS // 128) + i
            for half in range(2):
                turned = jnp.transpose(big[i * 128:(i + 1) * 128, half * DEV:(half + 1) * DEV])
                flat[pl.ds(half * (HALF_CAP // 2) + kp, DEV, stride=ROWS_F), :] = turned

    f_part[...] = flat[...].reshape(DEV, ROWS_F, 128).astype(BF16)


def slot_rows(slots):
    table = jnp.transpose(slots[:, 0, :].astype(F32)).astype(I32)
    rows = [table[k:k + 1] for k in range(CAP_F + CAP_C)]
    return jnp.concatenate(rows[:CAP_F], axis=1), jnp.concatenate(rows[CAP_F:], axis=1)


def reply_kernel(slots, fm, cm, f_part, c_part, out_ref, f_flat, c_flat, stage, sems):
    f_row, c_row = slot_rows(slots)
    f_vec = pick_fine(half_stack(fm[...]), one_hot(f_row & 255, 256), f_row)
    c_vec = mm(cm[...], one_hot(c_row, 64))

    def turned(vec, kp):
        at = 2 * kp * DEV
        return jnp.transpose(
            jnp.concatenate([vec[:, at:at + DEV], vec[:, at + DEV:at + 2 * DEV]], axis=0)
        )

    for kp in range(ROWS_F):
        f_flat[pl.ds(kp, DEV, stride=ROWS_F), :] = turned(f_vec, kp)
    for kp in range(ROWS_C):
        c_flat[pl.ds(kp, DEV, stride=2 * ROWS_C), :] = turned(c_vec, kp)
        c_flat[pl.ds(ROWS_C + kp, DEV, stride=2 * ROWS_C), :] = c_part[kp]
    each = DEV // SENDS
    copies = []
    for q in range(SENDS):
        devices = pl.ds(q * each, each)
        f_rows = f_flat[pl.ds(q * each * ROWS_F, each * ROWS_F), :]
        c_rows = c_flat[pl.ds(q * each * 2 * ROWS_C, each * 2 * ROWS_C), :]
        stage[devices] = jnp.concatenate(
            [
                f_rows.reshape(each, ROWS_F, 128).astype(BF16),
                f_part[devices],
                c_rows.reshape(each, 2 * ROWS_C, 128).astype(BF16),
            ],
            axis=1,
        )
        copies.append(pltpu.make_async_copy(stage.at[devices], out_ref.at[devices], sems.at[q]))
        copies[-1].start()
    for copy in copies:
        copy.wait()


def near_kernel(
    ops_in, s_nf, s_nc, fm, cm, f_boxes, c_boxes, f_out, c_out, ops, kinds, kf, sel, f_sum, sems
):
    copies = operator_copies(ops_in, ops, sems)
    for copy in copies:
        copy.start()
    kinds[0:G_NEAR_F] = s_nf[...]
    kinds[G_NEAR_F:NEAR_GROUPS] = s_nc[...]
    pick_operators(copies, ops, kinds, kf, sel)
    stack = half_stack(fm[...])
    f_sum[...] = jnp.zeros_like(f_sum)

    def step(i, carry):
        lanes = pl.ds(pl.multiple_of(i * NEAR_BLOCK, NEAR_BLOCK), NEAR_BLOCK)
        first = f_boxes[0:1, lanes]
        second = f_boxes[1:2, lanes]
        hot_1 = one_hot(first & 255, 256)
        hot_2 = one_hot(second & 255, 256)
        vec_1 = pick_fine(stack, hot_1, first).astype(BF16)
        vec_2 = pick_fine(stack, hot_2, second).astype(BF16)
        to_1, to_2 = [], []
        for k in range(NEAR_BLOCK // 128):
            op = sel[NEAR_BLOCK // 128 * i + k]
            cut = slice(k * 128, (k + 1) * 128)
            to_1.append(mm(op, vec_2[:, cut]))
            to_2.append(mm_tn(op, vec_1[:, cut]))
        to_1 = jnp.concatenate(to_1, axis=1)
        to_2 = jnp.concatenate(to_2, axis=1)
        both = jnp.concatenate([spread_fine(to_1, first), spread_fine(to_2, second)], axis=1)
        hots = jnp.concatenate([hot_1, hot_2], axis=1)
        f_sum[...] += mm_nt(both, hots)
        return carry

    lax.fori_loop(0, G_NEAR_F * 128 // NEAR_BLOCK, step, 0)
    f_out[...] = f_sum[:2 * RANK] + f_sum[2 * RANK:]
    total = jnp.zeros((2 * RANK, 64), F32)
    for g in range(G_NEAR_C):
        lanes = slice(g * 128, (g + 1) * 128)
        hot_1 = one_hot(c_boxes[0:1, lanes], 64)
        hot_2 = one_hot(c_boxes[1:2, lanes], 64)
        vec_1 = mm(cm[...], hot_1).astype(BF16)
        vec_2 = mm(cm[...], hot_2).astype(BF16)
        op = sel[G_NEAR_F + g]
        total = total + mm_nt(split_rows(mm(op, vec_2)), hot_1)
        total = total + mm_nt(split_rows(mm_tn(op, vec_1)), hot_2)
    c_out[...] = total[:RANK] + total[RANK:]


def final_kernel(
    got, slots, sel, f_near, c_near, parent, maps, f_owner, f_boxes, f_pos, c_owner, c_boxes, c_pos,
    c_ref, f_ref, flat,
):
    flat[...] = got[...].astype(F32).reshape(DEV * ROWS, 128)
    f_row, c_row = slot_rows(slots)

    def turned(row):
        return jnp.transpose(flat[pl.ds(row, DEV, stride=ROWS), :])

    def choose(found, where, count):
        vec = found[:RANK]
        for k in range(1, count):
            vec = jnp.where(where == k, found[k * RANK:(k + 1) * RANK], vec)
        return vec.astype(BF16)

    held_c = jnp.concatenate([turned(2 * ROWS_F + kp) for kp in range(ROWS_C)], axis=0)
    vec_c = choose(mm(held_c.astype(BF16), one_hot(c_owner[...], DEV)), c_pos[...], CAP_C)
    to_1 = jnp.concatenate(
        [mm(sel[G_FAR_F + g], vec_c[:, g * 128:(g + 1) * 128]) for g in range(G_FAR_C)], axis=1
    )
    far_c = mm_nt(split_rows(to_1), one_hot(c_boxes[0:1, :], 64))
    sides_c = []
    for kp in range(ROWS_C):
        arrived = turned(2 * ROWS_F + ROWS_C + kp)
        sides_c += [arrived[:RANK], arrived[RANK:]]
    arrived_c = mm_nt(jnp.concatenate(sides_c, axis=1).astype(BF16), one_hot(c_row, 64))
    coarse = parent[...] + c_near[...] + far_c[:RANK] + far_c[RANK:] + arrived_c
    coarse = coarse.astype(BF16)
    c_ref[...] = coarse

    held = jnp.concatenate(
        [
            jnp.concatenate([turned(quarter * (ROWS_F // 4) + kp) for quarter in range(4)], axis=1)
            for kp in range(ROWS_F // 4)
        ],
        axis=0,
    ).astype(BF16)
    pos = f_pos[...]
    hot = one_hot_wide((pos // PART_CAP) * DEV + f_owner[...], 4 * DEV)
    vec = choose(mm(held, hot), pos & (PART_CAP - 1), PART_CAP)
    to_1 = jnp.concatenate(
        [mm(sel[g], vec[:, g * 128:(g + 1) * 128]) for g in range(G_FAR_F)], axis=1
    )
    first = f_boxes[0:1, :]
    total = mm_nt(spread_fine(to_1, first), one_hot(first & 255, 256))
    sides = []
    for kp in range(ROWS_F):
        arrived = turned(ROWS_F + kp)
        sides += [arrived[:RANK], arrived[RANK:]]
    side = jnp.concatenate(sides, axis=1)
    side = jnp.concatenate(
        [jnp.where(f_row < 256, side, 0.0), jnp.where(f_row < 256, 0.0, side)], axis=0
    )
    added = mm_nt(side.astype(BF16), one_hot(f_row & 255, 256))

    box = lax.broadcasted_iota(I32, (64, 512), 1)
    parent_of = jnp.where((box >> 3) == lax.broadcasted_iota(I32, (64, 512), 0), 1.0, 0.0)
    wide = mm(coarse, parent_of.astype(BF16)).astype(BF16)
    starts = mm(maps[...].reshape(8 * RANK, RANK), wide)
    start = starts[:RANK]
    for k in range(1, 8):
        start = jnp.where((box & 7) == k, starts[k * RANK:(k + 1) * RANK], start)

    total = 2.0 * (f_near[...] + total[:2 * RANK] + total[2 * RANK:]) + added
    fine = start + jnp.concatenate([total[:RANK], total[RANK:]], axis=1)
    f_ref[...] = fine.astype(BF16)


def call(kernel, out_shape, scratch, mib, flops, nbytes, *args, **more):
    return pl.pallas_call(
        kernel,
        out_shape=out_shape,
        scratch_shapes=scratch,
        compiler_params=pltpu.CompilerParams(vmem_limit_bytes=mib * 1024 * 1024),
        cost_estimate=pl.CostEstimate(flops=flops, bytes_accessed=nbytes, transcendentals=0),
        **more,
    )(*args)


def on_device(
    coarse_multipole,
    fine_multipole,
    parent_local,
    operators,
    child_maps,
    coarse_near_boxes,
    coarse_near_shift,
    coarse_far_boxes,
    coarse_far_owner,
    coarse_far_shift,
    fine_near_boxes,
    fine_near_shift,
    fine_far_boxes,
    fine_far_owner,
    fine_far_shift,
):
    def sds(shape, dtype):
        return jax.ShapeDtypeStruct(shape, dtype)

    def in_hbm(x):
        return pltpu.with_memory_space_constraint(x, pltpu.HBM)

    fm, cm = fine_multipole, coarse_multipole
    vmem = pl.BlockSpec(memory_space=pltpu.VMEM)
    hbm = pl.BlockSpec(memory_space=pltpu.HBM)
    f_owner, c_owner = fine_far_owner.T, coarse_far_owner.T
    f_far, c_far = fine_far_boxes.T, coarse_far_boxes.T
    ops = in_hbm(jnp.transpose(operators, (1, 2, 0)))

    n_f, n_c = f_owner.shape[1], c_owner.shape[1]
    slots, f_pos, c_pos, f_owner, f_far, c_owner, c_far = call(
        route_kernel,
        (
            sds((DEV, 1, 128), I32),
            pltpu.VMEM((1, n_f), I32),
            pltpu.VMEM((1, n_c), I32),
            pltpu.VMEM((1, n_f), I32),
            pltpu.VMEM((2, n_f), I32),
            pltpu.VMEM((1, n_c), I32),
            pltpu.VMEM((2, n_c), I32),
        ),
        [pltpu.SemaphoreType.DMA((4,))],
        MIB_1,
        10**9,
        10**6,
        *[in_hbm(x) for x in (f_owner, f_far, c_owner, c_far)],
        in_specs=[hbm] * 4,
    )
    asked = lax.all_to_all(slots, ("oct", "box"), split_axis=0, concat_axis=0, tiled=True)
    sel, f_part, c_part = call(
        outgoing_kernel,
        (
            sds((FAR_GROUPS, RANK, RANK), BF16),
            sds((DEV, ROWS_F, 128), BF16),
            sds((ROWS_C, DEV, 128), F32),
        ),
        [
            pltpu.VMEM(ops.shape, BF16),
            pltpu.VMEM((RANK, n_f), BF16),
            pltpu.VMEM((RANK, n_c), BF16),
            pltpu.VMEM((FAR_GROUPS, 128), I32),
            pltpu.VMEM((FAR_GROUPS * RANK, RANK), F32),
            pltpu.VMEM((HALF_CAP * RANK, n_f), BF16),
            pltpu.VMEM((2 * DEV, n_f), BF16),
            pltpu.VMEM((DEV * ROWS_F, 128), F32),
            pltpu.SemaphoreType.DMA((OPS_CHUNKS,)),
        ],
        MIB_2,
        5 * 10**9,
        10**7,
        ops,
        fine_far_shift.reshape(-1, 128),
        coarse_far_shift.reshape(-1, 128),
        fm, cm, f_owner, f_far, f_pos, c_owner, c_far, c_pos,
        in_specs=[hbm] + [vmem] * 10,
    )
    sent = call(
        reply_kernel,
        pltpu.HBM((DEV, ROWS, 128), BF16),
        [
            pltpu.VMEM((DEV * ROWS_F, 128), F32),
            pltpu.VMEM((DEV * 2 * ROWS_C, 128), F32),
            pltpu.VMEM((DEV, ROWS, 128), BF16),
            pltpu.SemaphoreType.DMA((SENDS,)),
        ],
        MIB_3,
        10**9,
        10**6,
        asked, fm, cm, f_part, c_part,
        in_specs=[vmem] * 5,
        out_specs=hbm,
    )
    got = lax.all_to_all(sent, ("oct", "box"), split_axis=0, concat_axis=0, tiled=True)
    f_near, c_near = call(
        near_kernel,
        (sds((2 * RANK, 256), F32), sds((RANK, 64), F32)),
        [
            pltpu.VMEM(ops.shape, BF16),
            pltpu.VMEM((NEAR_GROUPS, 128), I32),
            pltpu.VMEM((NEAR_GROUPS * RANK, RANK), F32),
            pltpu.VMEM((NEAR_GROUPS, RANK, RANK), BF16),
            pltpu.VMEM((4 * RANK, 256), F32),
            pltpu.SemaphoreType.DMA((OPS_CHUNKS,)),
        ],
        MIB_4,
        10**10,
        10**7,
        ops,
        fine_near_shift.reshape(-1, 128),
        coarse_near_shift.reshape(-1, 128),
        fm, cm, fine_near_boxes.T, coarse_near_boxes.T,
        in_specs=[hbm] + [vmem] * 6,
    )
    return call(
        final_kernel,
        (sds((RANK, 64), BF16), sds((RANK, 512), BF16)),
        [pltpu.VMEM((DEV * ROWS, 128), F32)],
        MIB_5,
        3 * 10**9,
        10**7,
        got, asked, sel, f_near, c_near, parent_local, child_maps,
        f_owner, f_far, f_pos, c_owner, c_far, c_pos,
    )


def solution(mesh):
    both = ("oct", "box")
    return jax.shard_map(
        on_device,
        mesh=mesh,
        in_specs=(
            P(None, both),
            P(None, both),
            P(None, both),
            P(),
            P(),
            P(both, None),
            P(both),
            P(both, None),
            P(both, None),
            P(both),
            P(both, None),
            P(both),
            P(both, None),
            P(both, None),
            P(both),
        ),
        out_specs=(P(None, both), P(None, both)),
        check_vma=False,
    )
```

```python
import jax
import jax.numpy as jnp
from jax import lax
from jax.experimental import pallas as pl
from jax.experimental.pallas import tpu as pltpu
from jax.sharding import PartitionSpec as P


F32 = jnp.float32
BF16 = jnp.bfloat16
I32 = jnp.int32

DEV = 128
RANK = 64
CAP_F = 32
CAP_C = 8
ROWS_F = CAP_F * RANK // 128
ROWS_C = CAP_C * RANK // 128
ROWS = 2 * (ROWS_F + ROWS_C)
HALF_CAP = CAP_F // 2
PART_CAP = CAP_F // 4
G_NEAR_F, G_FAR_F, G_NEAR_C, G_FAR_C = 64, 16, 8, 4
FAR_GROUPS = 24
NEAR_GROUPS = G_NEAR_F + G_NEAR_C
NEAR_BLOCK = 4096
PM_ROWS = 512
OPS_CHUNKS = 2
SENDS = 8
MIB_1, MIB_2, MIB_3, MIB_4, MIB_5 = 16, 36, 24, 44, 40


def mm(a, b):
    return lax.dot_general(a, b, (((1,), (0,)), ((), ())), preferred_element_type=F32)


def mm_nt(a, b):
    return lax.dot_general(a, b, (((1,), (1,)), ((), ())), preferred_element_type=F32)


def mm_tn(a, b):
    return lax.dot_general(a, b, (((0,), (0,)), ((), ())), preferred_element_type=F32)


def one_hot(row, count):
    n = row.shape[1]
    at = lax.broadcasted_iota(I32, (count, n), 0).astype(BF16)
    hit = at == jnp.broadcast_to(row.astype(BF16), (count, n))
    return jnp.where(hit, jnp.ones((), BF16), jnp.zeros((), BF16))


def one_hot_wide(row, count):
    return jnp.concatenate(
        [one_hot(jnp.clip(row - at, -1, 256), 256) for at in range(0, count, 256)], axis=0
    )


def half_stack(m):
    return jnp.concatenate([m[:, :256], m[:, 256:]], axis=0)


def pick_fine(stack, hot, row):
    both = mm(stack, hot)
    return jnp.where(row < 256, both[:RANK], both[RANK:])


def split_rows(values):
    high = values.astype(BF16)
    low = (values - high.astype(F32)).astype(BF16)
    return jnp.concatenate([high, low], axis=0)


def spread_fine(values, row):
    first = jnp.where(row < 256, values, 0.0)
    second = jnp.where(row < 256, 0.0, values)
    return split_rows(jnp.concatenate([first, second], axis=0))


def prefix_matrix():
    down = lax.broadcasted_iota(I32, (128, 128), 0)
    across = lax.broadcasted_iota(I32, (128, 128), 1)
    return jnp.where(down <= across, 1.0, 0.0).astype(BF16)


def route_kernel(
    f_owner_in, f_boxes_in, c_owner_in, c_boxes_in,
    slots_ref, f_pos, c_pos, f_owner, f_boxes, c_owner, c_boxes, sems,
):
    copies = [
        pltpu.make_async_copy(source, target, sems.at[i])
        for i, (source, target) in enumerate(
            [
                (f_owner_in, f_owner),
                (c_owner_in, c_owner),
                (f_boxes_in, f_boxes),
                (c_boxes_in, c_boxes),
            ]
        )
    ]
    for copy in copies:
        copy.start()
    for copy in copies:
        copy.wait()
    f_blocks, c_blocks = f_owner.shape[1] // 128, c_owner.shape[1] // 128
    hits = [
        lax.broadcasted_iota(I32, (DEV, 128), 0) == ref[:, b * 128:(b + 1) * 128]
        for ref, blocks in ((f_owner, f_blocks), (c_owner, c_blocks))
        for b in range(blocks)
    ]
    hots = [jnp.where(hit, 1.0, 0.0).astype(BF16) for hit in hits]
    counts = mm(jnp.concatenate(hots, axis=0), prefix_matrix())

    def place(boxes_ref, pos_ref, start, blocks, cap, wide):
        carry = jnp.zeros((DEV, 128), F32)
        parts = []
        for b in range(blocks):
            lanes = slice(b * 128, (b + 1) * 128)
            count = counts[(start + b) * 128:(start + b + 1) * 128]
            seen = count + carry
            pos = jnp.sum(jnp.where(hits[start + b], seen, 0.0), axis=0, keepdims=True) - 1.0
            carry = carry + jnp.broadcast_to(count[:, 127:128], (DEV, 128))
            pos = pos.astype(I32)
            pos_ref[:, lanes] = pos
            slot = boxes_ref[1:2, lanes]
            here = lax.broadcasted_iota(I32, (cap, 128), 0) == pos
            low = jnp.where(here, (slot & 255).astype(F32), 0.0)
            if wide:
                high = jnp.where(here, (slot >> 8).astype(F32), 0.0)
                low = jnp.concatenate([low, high], axis=0)
            parts.append(low.astype(BF16))
        table = mm_nt(
            jnp.concatenate(parts, axis=1), jnp.concatenate(hots[start:start + blocks], axis=1)
        )
        if wide:
            table = table[:cap] + 256.0 * table[cap:]
        return table

    fine = place(f_boxes, f_pos, 0, f_blocks, CAP_F, True)
    coarse = place(c_boxes, c_pos, f_blocks, c_blocks, CAP_C, False)
    rest = jnp.zeros((128 - CAP_F - CAP_C, DEV), F32)
    table = jnp.concatenate([fine, coarse, rest], axis=0)
    slots_ref[:, 0, :] = jnp.transpose(table).astype(I32)


def operator_copies(ops_in, ops, sems):
    each = RANK // OPS_CHUNKS
    return [
        pltpu.make_async_copy(
            ops_in.at[pl.ds(k * each, each)], ops.at[pl.ds(k * each, each)], sems.at[k]
        )
        for k in range(OPS_CHUNKS)
    ]


def pick_operators(copies, ops, kinds, flat, out):
    groups, nt = kinds.shape[0], ops.shape[2]
    hot = jnp.where(kinds[:, 0:1] == lax.broadcasted_iota(I32, (groups, nt), 1), 1.0, 0.0)
    hot = hot.astype(BF16)
    for quad in range(RANK // 4):
        if quad % (RANK // 4 // OPS_CHUNKS) == 0:
            copies[quad // (RANK // 4 // OPS_CHUNKS)].wait()
        rows = ops[quad * 4:(quad + 1) * 4].reshape(256, nt)
        got = mm_nt(hot, rows)
        for k in range(4):
            flat[pl.ds(quad * 4 + k, groups, stride=RANK), :] = got[:, k * RANK:(k + 1) * RANK]
    out[...] = flat[...].reshape(groups, RANK, RANK).astype(BF16)


def outgoing_kernel(
    ops_in, s_ff, s_fc, fm, cm, f_owner, f_boxes, f_pos, c_owner, c_boxes, c_pos,
    sel_ref, f_part, c_part, ops, f_vec, c_vec, kinds, kf, pm, hot_out, flat, sems,
):
    copies = operator_copies(ops_in, ops, sems)
    for copy in copies:
        copy.start()
    row = f_boxes[0:1, :]
    f_vec[...] = pick_fine(half_stack(fm[...]), one_hot(row & 255, 256), row).astype(BF16)
    c_vec[...] = mm(cm[...], one_hot(c_boxes[0:1, :], 64)).astype(BF16)
    pos = f_pos[...]
    hot_out[...] = one_hot((pos >> 4) * DEV + f_owner[...], 2 * DEV)
    kinds[...] = jnp.zeros_like(kinds)
    kinds[0:G_FAR_F] = s_ff[...]
    kinds[G_FAR_F:G_FAR_F + G_FAR_C] = s_fc[...]
    pick_operators(copies, ops, kinds, kf, sel_ref)

    part = jnp.concatenate(
        [
            mm_tn(sel_ref[G_FAR_F + g], c_vec[:, g * 128:(g + 1) * 128])
            for g in range(G_FAR_C)
        ],
        axis=1,
    )
    at = c_pos[...]
    pieces = [jnp.where(at == k, part, 0.0).astype(BF16) for k in range(CAP_C)]
    big = mm_nt(jnp.concatenate(pieces, axis=0), one_hot(c_owner[...], DEV))
    for kp in range(ROWS_C):
        c_part[kp] = jnp.transpose(big[kp * 128:(kp + 1) * 128])

    part = jnp.concatenate(
        [mm_tn(sel_ref[g], f_vec[:, g * 128:(g + 1) * 128]) for g in range(G_FAR_F)], axis=1
    )
    part = (2.0 * part).astype(BF16)
    step = jnp.broadcast_to((pos & (HALF_CAP - 1)).astype(BF16), part.shape)
    none = jnp.zeros((), BF16)
    for k in range(HALF_CAP):
        pm[k * RANK:(k + 1) * RANK, :] = jnp.where(step == jnp.asarray(k, BF16), part, none)
    for j in range(HALF_CAP * RANK // PM_ROWS):
        big = mm_nt(pm[j * PM_ROWS:(j + 1) * PM_ROWS, :], hot_out[...])
        for i in range(PM_ROWS // 128):
            kp = j * (PM_ROWS // 128) + i
            for half in range(2):
                turned = jnp.transpose(big[i * 128:(i + 1) * 128, half * DEV:(half + 1) * DEV])
                flat[pl.ds(half * (HALF_CAP // 2) + kp, DEV, stride=ROWS_F), :] = turned

    f_part[...] = flat[...].reshape(DEV, ROWS_F, 128).astype(BF16)


def slot_rows(slots):
    table = jnp.transpose(slots[:, 0, :].astype(F32)).astype(I32)
    rows = [table[k:k + 1] for k in range(CAP_F + CAP_C)]
    return jnp.concatenate(rows[:CAP_F], axis=1), jnp.concatenate(rows[CAP_F:], axis=1)


def reply_kernel(slots, fm, cm, f_part, c_part, out_ref, f_flat, c_flat, stage, sems):
    f_row, c_row = slot_rows(slots)
    f_vec = pick_fine(half_stack(fm[...]), one_hot(f_row & 255, 256), f_row)
    c_vec = mm(cm[...], one_hot(c_row, 64))

    def turned(vec, kp):
        at = 2 * kp * DEV
        return jnp.transpose(
            jnp.concatenate([vec[:, at:at + DEV], vec[:, at + DEV:at + 2 * DEV]], axis=0)
        )

    for kp in range(ROWS_F):
        f_flat[pl.ds(kp, DEV, stride=ROWS_F), :] = turned(f_vec, kp)
    for kp in range(ROWS_C):
        c_flat[pl.ds(kp, DEV, stride=2 * ROWS_C), :] = turned(c_vec, kp)
        c_flat[pl.ds(ROWS_C + kp, DEV, stride=2 * ROWS_C), :] = c_part[kp]
    each = DEV // SENDS
    copies = []
    for q in range(SENDS):
        devices = pl.ds(q * each, each)
        f_rows = f_flat[pl.ds(q * each * ROWS_F, each * ROWS_F), :]
        c_rows = c_flat[pl.ds(q * each * 2 * ROWS_C, each * 2 * ROWS_C), :]
        stage[devices] = jnp.concatenate(
            [
                f_rows.reshape(each, ROWS_F, 128).astype(BF16),
                f_part[devices],
                c_rows.reshape(each, 2 * ROWS_C, 128).astype(BF16),
            ],
            axis=1,
        )
        copies.append(pltpu.make_async_copy(stage.at[devices], out_ref.at[devices], sems.at[q]))
        copies[-1].start()
    for copy in copies:
        copy.wait()


def near_kernel(
    ops_in, s_nf, s_nc, fm, cm, f_boxes, c_boxes, f_out, c_out, ops, kinds, kf, sel, f_sum, sems
):
    copies = operator_copies(ops_in, ops, sems)
    for copy in copies:
        copy.start()
    kinds[0:G_NEAR_F] = s_nf[...]
    kinds[G_NEAR_F:NEAR_GROUPS] = s_nc[...]
    pick_operators(copies, ops, kinds, kf, sel)
    stack = half_stack(fm[...])
    f_sum[...] = jnp.zeros_like(f_sum)

    def step(i, carry):
        lanes = pl.ds(pl.multiple_of(i * NEAR_BLOCK, NEAR_BLOCK), NEAR_BLOCK)
        first = f_boxes[0:1, lanes]
        second = f_boxes[1:2, lanes]
        hot_1 = one_hot(first & 255, 256)
        hot_2 = one_hot(second & 255, 256)
        vec_1 = pick_fine(stack, hot_1, first).astype(BF16)
        vec_2 = pick_fine(stack, hot_2, second).astype(BF16)
        to_1, to_2 = [], []
        for k in range(NEAR_BLOCK // 128):
            op = sel[NEAR_BLOCK // 128 * i + k]
            cut = slice(k * 128, (k + 1) * 128)
            to_1.append(mm(op, vec_2[:, cut]))
            to_2.append(mm_tn(op, vec_1[:, cut]))
        to_1 = jnp.concatenate(to_1, axis=1)
        to_2 = jnp.concatenate(to_2, axis=1)
        both = jnp.concatenate([spread_fine(to_1, first), spread_fine(to_2, second)], axis=1)
        hots = jnp.concatenate([hot_1, hot_2], axis=1)
        f_sum[...] += mm_nt(both, hots)
        return carry

    lax.fori_loop(0, G_NEAR_F * 128 // NEAR_BLOCK, step, 0)
    f_out[...] = f_sum[:2 * RANK] + f_sum[2 * RANK:]
    total = jnp.zeros((2 * RANK, 64), F32)
    for g in range(G_NEAR_C):
        lanes = slice(g * 128, (g + 1) * 128)
        hot_1 = one_hot(c_boxes[0:1, lanes], 64)
        hot_2 = one_hot(c_boxes[1:2, lanes], 64)
        vec_1 = mm(cm[...], hot_1).astype(BF16)
        vec_2 = mm(cm[...], hot_2).astype(BF16)
        op = sel[G_NEAR_F + g]
        total = total + mm_nt(split_rows(mm(op, vec_2)), hot_1)
        total = total + mm_nt(split_rows(mm_tn(op, vec_1)), hot_2)
    c_out[...] = total[:RANK] + total[RANK:]


def final_kernel(
    got, slots, sel, f_near, c_near, parent, maps, f_owner, f_boxes, f_pos, c_owner, c_boxes, c_pos,
    c_ref, f_ref, flat,
):
    flat[...] = got[...].astype(F32).reshape(DEV * ROWS, 128)
    f_row, c_row = slot_rows(slots)

    def turned(row):
        return jnp.transpose(flat[pl.ds(row, DEV, stride=ROWS), :])

    def choose(found, where, count):
        vec = found[:RANK]
        for k in range(1, count):
            vec = jnp.where(where == k, found[k * RANK:(k + 1) * RANK], vec)
        return vec.astype(BF16)

    held_c = jnp.concatenate([turned(2 * ROWS_F + kp) for kp in range(ROWS_C)], axis=0)
    vec_c = choose(mm(held_c.astype(BF16), one_hot(c_owner[...], DEV)), c_pos[...], CAP_C)
    to_1 = jnp.concatenate(
        [mm(sel[G_FAR_F + g], vec_c[:, g * 128:(g + 1) * 128]) for g in range(G_FAR_C)], axis=1
    )
    far_c = mm_nt(split_rows(to_1), one_hot(c_boxes[0:1, :], 64))
    sides_c = []
    for kp in range(ROWS_C):
        arrived = turned(2 * ROWS_F + ROWS_C + kp)
        sides_c += [arrived[:RANK], arrived[RANK:]]
    arrived_c = mm_nt(jnp.concatenate(sides_c, axis=1).astype(BF16), one_hot(c_row, 64))
    coarse = parent[...] + c_near[...] + far_c[:RANK] + far_c[RANK:] + arrived_c
    coarse = coarse.astype(BF16)
    c_ref[...] = coarse

    held = jnp.concatenate(
        [
            jnp.concatenate([turned(quarter * (ROWS_F // 4) + kp) for quarter in range(4)], axis=1)
            for kp in range(ROWS_F // 4)
        ],
        axis=0,
    ).astype(BF16)
    pos = f_pos[...]
    hot = one_hot_wide((pos // PART_CAP) * DEV + f_owner[...], 4 * DEV)
    vec = choose(mm(held, hot), pos & (PART_CAP - 1), PART_CAP)
    to_1 = jnp.concatenate(
        [mm(sel[g], vec[:, g * 128:(g + 1) * 128]) for g in range(G_FAR_F)], axis=1
    )
    first = f_boxes[0:1, :]
    total = mm_nt(spread_fine(to_1, first), one_hot(first & 255, 256))
    sides = []
    for kp in range(ROWS_F):
        arrived = turned(ROWS_F + kp)
        sides += [arrived[:RANK], arrived[RANK:]]
    side = jnp.concatenate(sides, axis=1)
    side = jnp.concatenate(
        [jnp.where(f_row < 256, side, 0.0), jnp.where(f_row < 256, 0.0, side)], axis=0
    )
    added = mm_nt(side.astype(BF16), one_hot(f_row & 255, 256))

    box = lax.broadcasted_iota(I32, (64, 512), 1)
    parent_of = jnp.where((box >> 3) == lax.broadcasted_iota(I32, (64, 512), 0), 1.0, 0.0)
    wide = mm(coarse, parent_of.astype(BF16)).astype(BF16)
    starts = mm(maps[...].reshape(8 * RANK, RANK), wide)
    start = starts[:RANK]
    for k in range(1, 8):
        start = jnp.where((box & 7) == k, starts[k * RANK:(k + 1) * RANK], start)

    total = 2.0 * (f_near[...] + total[:2 * RANK] + total[2 * RANK:]) + added
    fine = start + jnp.concatenate([total[:RANK], total[RANK:]], axis=1)
    f_ref[...] = fine.astype(BF16)


def call(kernel, out_shape, scratch, mib, flops, nbytes, *args, **more):
    return pl.pallas_call(
        kernel,
        out_shape=out_shape,
        scratch_shapes=scratch,
        compiler_params=pltpu.CompilerParams(vmem_limit_bytes=mib * 1024 * 1024),
        cost_estimate=pl.CostEstimate(flops=flops, bytes_accessed=nbytes, transcendentals=0),
        **more,
    )(*args)


def on_device(
    coarse_multipole,
    fine_multipole,
    parent_local,
    operators,
    child_maps,
    coarse_near_boxes,
    coarse_near_shift,
    coarse_far_boxes,
    coarse_far_owner,
    coarse_far_shift,
    fine_near_boxes,
    fine_near_shift,
    fine_far_boxes,
    fine_far_owner,
    fine_far_shift,
):
    def sds(shape, dtype):
        return jax.ShapeDtypeStruct(shape, dtype)

    def in_hbm(x):
        return pltpu.with_memory_space_constraint(x, pltpu.HBM)

    fm, cm = fine_multipole, coarse_multipole
    vmem = pl.BlockSpec(memory_space=pltpu.VMEM)
    hbm = pl.BlockSpec(memory_space=pltpu.HBM)
    f_owner, c_owner = fine_far_owner.T, coarse_far_owner.T
    f_far, c_far = fine_far_boxes.T, coarse_far_boxes.T
    ops = in_hbm(jnp.transpose(operators, (1, 2, 0)))

    n_f, n_c = f_owner.shape[1], c_owner.shape[1]
    slots, f_pos, c_pos, f_owner, f_far, c_owner, c_far = call(
        route_kernel,
        (
            sds((DEV, 1, 128), I32),
            pltpu.VMEM((1, n_f), I32),
            pltpu.VMEM((1, n_c), I32),
            pltpu.VMEM((1, n_f), I32),
            pltpu.VMEM((2, n_f), I32),
            pltpu.VMEM((1, n_c), I32),
            pltpu.VMEM((2, n_c), I32),
        ),
        [pltpu.SemaphoreType.DMA((4,))],
        MIB_1,
        10**9,
        10**6,
        *[in_hbm(x) for x in (f_owner, f_far, c_owner, c_far)],
        in_specs=[hbm] * 4,
    )
    asked = lax.all_to_all(slots, ("oct", "box"), split_axis=0, concat_axis=0, tiled=True)
    sel, f_part, c_part = call(
        outgoing_kernel,
        (
            sds((FAR_GROUPS, RANK, RANK), BF16),
            sds((DEV, ROWS_F, 128), BF16),
            sds((ROWS_C, DEV, 128), F32),
        ),
        [
            pltpu.VMEM(ops.shape, BF16),
            pltpu.VMEM((RANK, n_f), BF16),
            pltpu.VMEM((RANK, n_c), BF16),
            pltpu.VMEM((FAR_GROUPS, 128), I32),
            pltpu.VMEM((FAR_GROUPS * RANK, RANK), F32),
            pltpu.VMEM((HALF_CAP * RANK, n_f), BF16),
            pltpu.VMEM((2 * DEV, n_f), BF16),
            pltpu.VMEM((DEV * ROWS_F, 128), F32),
            pltpu.SemaphoreType.DMA((OPS_CHUNKS,)),
        ],
        MIB_2,
        5 * 10**9,
        10**7,
        ops,
        fine_far_shift.reshape(-1, 128),
        coarse_far_shift.reshape(-1, 128),
        fm, cm, f_owner, f_far, f_pos, c_owner, c_far, c_pos,
        in_specs=[hbm] + [vmem] * 10,
    )
    sent = call(
        reply_kernel,
        pltpu.HBM((DEV, ROWS, 128), BF16),
        [
            pltpu.VMEM((DEV * ROWS_F, 128), F32),
            pltpu.VMEM((DEV * 2 * ROWS_C, 128), F32),
            pltpu.VMEM((DEV, ROWS, 128), BF16),
            pltpu.SemaphoreType.DMA((SENDS,)),
        ],
        MIB_3,
        10**9,
        10**6,
        asked, fm, cm, f_part, c_part,
        in_specs=[vmem] * 5,
        out_specs=hbm,
    )
    got = lax.all_to_all(sent, ("oct", "box"), split_axis=0, concat_axis=0, tiled=True)
    f_near, c_near = call(
        near_kernel,
        (sds((2 * RANK, 256), F32), sds((RANK, 64), F32)),
        [
            pltpu.VMEM(ops.shape, BF16),
            pltpu.VMEM((NEAR_GROUPS, 128), I32),
            pltpu.VMEM((NEAR_GROUPS * RANK, RANK), F32),
            pltpu.VMEM((NEAR_GROUPS, RANK, RANK), BF16),
            pltpu.VMEM((4 * RANK, 256), F32),
            pltpu.SemaphoreType.DMA((OPS_CHUNKS,)),
        ],
        MIB_4,
        10**10,
        10**7,
        ops,
        fine_near_shift.reshape(-1, 128),
        coarse_near_shift.reshape(-1, 128),
        fm, cm, fine_near_boxes.T, coarse_near_boxes.T,
        in_specs=[hbm] + [vmem] * 6,
    )
    return call(
        final_kernel,
        (sds((RANK, 64), BF16), sds((RANK, 512), BF16)),
        [pltpu.VMEM((DEV * ROWS, 128), F32)],
        MIB_5,
        3 * 10**9,
        10**7,
        got, asked, sel, f_near, c_near, parent_local, child_maps,
        f_owner, f_far, f_pos, c_owner, c_far, c_pos,
    )


def solution(mesh):
    both = ("oct", "box")
    return jax.shard_map(
        on_device,
        mesh=mesh,
        in_specs=(
            P(None, both),
            P(None, both),
            P(None, both),
            P(),
            P(),
            P(both, None),
            P(both),
            P(both, None),
            P(both, None),
            P(both),
            P(both, None),
            P(both),
            P(both, None),
            P(both, None),
            P(both),
        ),
        out_specs=(P(None, both), P(None, both)),
        check_vma=False,
    )
```
